256 devices in a mesh: row: 32 (over y_lo, z, core), col: 8 (over y_hi, x).
Axes of the slice: x: 4, y: 4 (y_hi: 2, y_lo: 2; y = y_hi * 2 + y_lo), z: 8, core: 2. Of those that a mesh axis runs over, the one named last changes fastest.
Arguments:
- tokens: bfloat16 [16384, 5120], P('row'), may hold values from -6 to 6
- cotangent: bfloat16 [16384, 3072], P('row', 'col'), may hold values from -0.125 to 0.125
- teacher: bfloat16 [4096, 2048], P('row', 'col'), may hold values from -0.09375 to 0.09375
- expand_model: float32 [5120, 4096], P('row', 'col'), may hold values from -0.09375 to 0.09375
- expand_heads: float32 [3072, 2048], P('col', 'row'), may hold values from -0.125 to 0.125
Outputs:
- queries: float32 [16384, 3072], P('row', 'col')
- grad_model: float32 [5120, 4096], P('row', 'col')
- grad_heads: float32 [3072, 2048], P('col', 'row')
The draws below stay inside these ranges and needn't reach their ends.
All inputs are finite; a program needn't handle non-finite values.
Results may differ from the reference program's by a relative error of at most 0.0029.
Values may be sent and summed in bfloat16 or wider, within the bound.
No kernel may reach another device: no remote copies, remote signals or barrier semaphores. Data moves between devices by JAX's collectives and lax.ppermute only.
A program may use at most 128 MiB of HBM per device.

```python
import jax
import jax.numpy as jnp
from jax import lax

D1 = 4096
D2 = 5120
Q1 = 2048
Q2 = 3072
TOKENS = 16384


def with_spikes(drawn, rng, source, target, parts, factor):
    def block_of(dim):
        return (jnp.arange(drawn.shape[dim]) // (drawn.shape[dim] // parts)).reshape((-1,) + (1,) * (drawn.ndim - 1 - dim))

    near = jax.random.permutation(rng, parts)[block_of(target)]
    far = (block_of(target) + parts // 2) % parts
    return jnp.where((block_of(source) == near) | (block_of(source) == far), factor * drawn, drawn)


def steps_of(key, shape, cuts, smallest, top_value):
    factor_of = 1.0
    for dim, blocks in cuts:
        draws = jax.random.uniform(jax.random.fold_in(jax.random.fold_in(key, 6), dim), (blocks,), jnp.float32, smallest / len(cuts), top_value / len(cuts))
        factor_of = factor_of * jnp.repeat(jnp.exp(draws), shape[dim] // blocks).reshape((-1,) + (1,) * (len(shape) - 1 - dim))
    return factor_of


def gaussian(own_key, extent, deviation, bound, shards=(), kind=jnp.bfloat16):
    values = jax.random.normal(own_key, extent, jnp.float32) * deviation
    if len(shards) > 0:
        values = steps_of(own_key, extent, shards, -0.22, 0.18) * values
    return jnp.clip(values, min=-bound, max=bound).astype(kind)


def gaussian_with(own_key, shape, width, reach, split, heavy, dtype=jnp.bfloat16):
    entries = width * jax.random.normal(own_key, shape, jnp.float32)
    if split:
        entries = entries * steps_of(own_key, shape, split, -0.22, 0.18)
    return jnp.clip(with_spikes(entries, jax.random.fold_in(own_key, 3), *heavy), -reach, reach).astype(dtype)


def setup_inputs(seed: int = 0) -> dict:
    keys = jax.random.split(jax.random.key(seed), 6)
    tokens = gaussian_with(keys[0], (TOKENS, D2), 1.0, 6.0, ((0, 32),), (0, 1, 32, 2.75))
    cotangent = gaussian(keys[1], (TOKENS, Q2), (TOKENS ** -0.5), 0.125, ((0, 32), (1, 8)))
    teacher = gaussian(keys[2], (D1, Q1), D1 ** -0.5, 0.09375, ((0, 32), (1, 8)))
    expand_model = gaussian(keys[3], (D2, D1), D1 ** -0.5, 0.09375, ((0, 32), (1, 8)), jnp.float32)
    expand_heads = gaussian(keys[4], (Q2, Q1), Q1 ** -0.5, 0.125, ((0, 8), (1, 32)), jnp.float32)
    return {"tokens": tokens, "cotangent": cotangent, "teacher": teacher, "expand_model": expand_model, "expand_heads": expand_heads}


def reference(tokens, cotangent, teacher, expand_model, expand_heads):
    highest = lax.Precision.HIGHEST
    teacher_wide = teacher.astype(jnp.float32)
    expanded = jnp.dot(expand_model, teacher_wide, precision=highest)
    student = jnp.dot(expanded, expand_heads.T, precision=highest).astype(jnp.bfloat16)
    queries = jnp.dot(tokens, student, preferred_element_type=jnp.float32)
    weight_grad = jnp.dot(tokens.T, cotangent, preferred_element_type=jnp.float32)
    grad_heads = jnp.dot(weight_grad.T, expanded, precision=highest)
    side = jnp.dot(weight_grad, expand_heads, precision=highest)
    grad_model = jnp.dot(side, teacher_wide.T, precision=highest)
    return queries, grad_model, grad_heads
```

```python
import functools

import jax
import jax.numpy as jnp
from jax import lax
from jax.experimental import pallas as pl
from jax.experimental.pallas import tpu as pltpu
from jax.sharding import PartitionSpec as P

f32, f16, bf16 = jnp.float32, jnp.float16, jnp.bfloat16
HIGH = lax.Precision.HIGH
PAD = 8
TOP = 14.0


def row_perm(move):
    pairs = []
    for r in range(32):
        yl, z, c = move(r // 16, r // 2 % 8, r % 2)
        pairs.append((r, yl * 16 + z % 8 * 2 + c))
    return pairs


def hop_core(a):
    return lax.ppermute(a, "row", row_perm(lambda yl, z, c: (yl, z, 1 - c)))


def hop_y(a):
    return lax.ppermute(a, "row", row_perm(lambda yl, z, c: (1 - yl, z, c)))


def hop_z(a, d):
    return lax.ppermute(a, "row", row_perm(lambda yl, z, c: (yl, z + d, c)))


def hop_col(a, dyh, dx):
    return lax.ppermute(
        a, "col", [(q, (q // 4 + dyh) % 2 * 4 + (q % 4 + dx) % 4) for q in range(8)]
    )


def bound_of(x):
    return jnp.ceil(jnp.log2(jnp.maximum(jnp.max(jnp.abs(x)), 2.0**-100)))


def join(*ks):
    return jnp.ceil(jnp.log2(functools.reduce(jnp.add, [jnp.exp2(k) for k in ks])))


def enc(x, k):
    y = (x * jnp.exp2(TOP - k)).astype(f16)
    pad = jnp.broadcast_to(jnp.asarray(k, f16), x.shape[:-2] + (PAD, x.shape[-1]))
    return jnp.concatenate([y, pad], axis=-2)


def key(p):
    return p[..., -1:, :].astype(f32)


def dec(p):
    return p[..., :-PAD, :].astype(f32) * jnp.exp2(key(p) - TOP)


def place(where, parts):
    total = sum(p.shape[0] for p in parts)
    block = parts[0].shape[1:]

    def kernel(where_ref, *refs):
        out = refs[-1]
        n = 0
        for src in refs[:-1]:
            for j in range(src.shape[0]):
                out[where_ref[n]] = src[j]
                n += 1

    return pl.pallas_call(
        kernel,
        out_shape=jax.ShapeDtypeStruct((total,) + block, parts[0].dtype),
        in_specs=[pl.BlockSpec(memory_space=pltpu.SMEM)]
        + [pl.BlockSpec(memory_space=pltpu.VMEM)] * len(parts),
        out_specs=pl.BlockSpec(memory_space=pltpu.VMEM),
        compiler_params=pltpu.CompilerParams(vmem_limit_bytes=32 * 2**20),
    )(where, *parts)


def gather_row(a, yl, z, c):
    two = jnp.stack([a, hop_y(a)])
    from_m2 = hop_z(two, 2)
    from_p2 = hop_z(two, -2)
    from_m1 = hop_z(jnp.stack([two, from_m2]), 1)
    from_p1 = hop_z(jnp.stack([two, from_p2]), -1)
    half_0 = hop_z(from_m2[:1], 2)
    half_1 = hop_z(from_p2[1:], -2)
    mine = [two, from_m2, from_p2, from_m1.reshape((4,) + a.shape), from_p1.reshape((4,) + a.shape), half_0, half_1]
    offsets = [(0, 0), (1, 0), (0, -2), (1, -2), (0, 2), (1, 2), (0, -1), (1, -1), (0, -3), (1, -3), (0, 1), (1, 1), (0, 3), (1, 3), (0, 4), (1, 4)]
    mine = jnp.concatenate(mine)
    other = hop_core(mine)
    where = [(yl ^ j) * 16 + (z + d) % 8 * 2 + c for j, d in offsets]
    where += [(yl ^ j) * 16 + (z + d) % 8 * 2 + (1 - c) for j, d in offsets]
    return jnp.stack(where).astype(jnp.int32), [mine, other]


def scatter_row(w, yl, z, c):
    n, m = w.shape[0] // 32, w.shape[1]
    w = w.reshape(2, 8, 2, n, m)
    send = lax.dynamic_index_in_dim(w, 1 - c, 2, keepdims=False).astype(bf16)
    x = lax.dynamic_index_in_dim(w, c, 2, keepdims=False) + hop_core(send).astype(f32)
    k = bound_of(x)

    def part(d):
        return lax.dynamic_index_in_dim(x, (z + d) % 8, 1, keepdims=False)

    near = [jnp.concatenate([part(d), part(3 * d)]).reshape(4 * n, m) for d in (1, -1)]
    up1 = hop_z(enc(near[0], k), 1)
    dn1 = hop_z(enc(near[1], k), -1)
    far = part(4)
    up2 = hop_z(enc(far[0], k), 2)
    dn2 = hop_z(enc(far[1], k), -2)
    d_up1, d_dn1 = dec(up1).reshape(2, 2, n, m), dec(dn1).reshape(2, 2, n, m)
    zero = jnp.zeros((n, m), f32)
    m_up = part(2) + d_up1[1] + jnp.stack([dec(up2), zero])
    m_dn = part(-2) + d_dn1[1] + jnp.stack([zero, dec(dn2)])
    k_up = join(k, key(up1), key(up2))
    k_dn = join(k, key(dn1), key(dn2))
    r_up = hop_z(enc(m_up.reshape(2 * n, m), k_up), 2)
    r_dn = hop_z(enc(m_dn.reshape(2 * n, m), k_dn), -2)
    y = part(0) + d_up1[0] + d_dn1[0] + dec(r_up).reshape(2, n, m) + dec(r_dn).reshape(2, n, m)
    k_y = join(k, key(up1), key(dn1), key(r_up), key(r_dn))
    out = enc(lax.dynamic_index_in_dim(y, 1 - yl, 0, keepdims=False), k_y)
    return lax.dynamic_index_in_dim(y, yl, 0, keepdims=False) + dec(hop_y(out))


def gather_col(a, yh, x):
    two = jnp.stack([a, hop_col(a, 1, 0)])
    parts = [two] + [hop_col(two, 0, d) for d in (1, -1, 2)]
    where = [(yh ^ j) * 4 + (x - d) % 4 for d in (0, 1, -1, 2) for j in (0, 1)]
    return place(jnp.stack(where).astype(jnp.int32), [dec(p) for p in parts])


def scatter_col(a):
    n, m = a.shape[0], a.shape[1] // 8
    k = bound_of(a)
    blocks = enc(a.reshape(n, 8, m).transpose(1, 0, 2), k)
    return jnp.sum(dec(lax.all_to_all(blocks, "col", 0, 0, tiled=True)), axis=0)


def shards(tokens, cotangent, teacher, expand_model, expand_heads):
    r, q = lax.axis_index("row"), lax.axis_index("col")
    yl, z, c = r // 16, r // 2 % 8, r % 2
    yh, x = q // 4, q % 4

    weight = lax.dot_general(
        tokens, cotangent, (((0,), (0,)), ((), ())), preferred_element_type=f32
    )

    heads_t = expand_heads.T
    k_t, k_h = bound_of(teacher.astype(f32)), bound_of(heads_t)
    tail = jnp.concatenate([heads_t[:32, 256:], heads_t[32:, 256:]], axis=1)
    both = jnp.concatenate(
        [enc(teacher.astype(f32), k_t), enc(jnp.concatenate([heads_t[:, :256], tail]), k_h)]
    )
    where, both = gather_row(both, yl, z, c)
    teacher_block = place(where, [dec(p[:, : 128 + PAD]).astype(bf16) for p in both])
    teacher_block = teacher_block.reshape(4096, 256)
    heads = []
    for p in both:
        h = dec(p[:, 128 + PAD :])
        tail = jnp.concatenate([h[:, 64:, :128], h[:, 64:, 128:]], axis=1)
        heads.append(jnp.concatenate([h[:, :64], tail], axis=2))
    heads = place(where, heads).reshape(2048, 384)

    model = gather_col(enc(expand_model, bound_of(expand_model)), yh, x)
    model_rows = model.transpose(1, 0, 2).reshape(160, 4096)
    expanded = jnp.dot(model_rows, teacher_block.astype(f32), precision=HIGH)
    spread = jnp.broadcast_to(enc(expanded, bound_of(expanded)), (8, 160 + PAD, 256))
    expanded = dec(lax.all_to_all(spread, "col", 0, 0, tiled=True))
    expanded = expanded.transpose(1, 0, 2).reshape(160, 2048)
    student = jnp.dot(expanded, heads, precision=HIGH).astype(bf16)
    student = place(*gather_row(student, yl, z, c)).reshape(5120, 384)
    queries = jnp.dot(tokens, student, preferred_element_type=f32)

    grad = scatter_row(weight, yl, z, c)
    heads_share = lax.dot_general(
        expanded, grad, (((0,), (0,)), ((), ())), precision=HIGH, preferred_element_type=f32
    )
    grad_heads = scatter_row(heads_share, yl, z, c).T
    side = scatter_col(
        lax.dot_general(grad, heads, (((1,), (1,)), ((), ())), precision=HIGH)
    )
    grad_model = scatter_col(
        lax.dot_general(side, teacher_block.astype(f32), (((1,), (1,)), ((), ())), precision=HIGH)
    )
    return (queries, grad_model, grad_heads)


def solution(mesh):
    in_specs = (P("row", None), P("row", "col"), P("row", "col"), P("row", "col"), P("col", "row"))
    out_specs = (P("row", "col"), P("row", "col"), P("col", "row"))
    return jax.shard_map(shards, mesh=mesh, in_specs=in_specs, out_specs=out_specs, check_vma=False)
```

```python
import jax
import jax.numpy as jnp
from jax import lax
from jax.experimental import pallas as pl
from jax.experimental.pallas import tpu as pltpu
from jax.sharding import Mesh, PartitionSpec as P

f32, f16, bf16 = jnp.float32, jnp.float16, jnp.bfloat16
HIGH = lax.Precision.HIGH
PAD = 8
TOP = 14.0
ROW, COL, CHIPS = ("yl", "z", "c"), ("yh", "x"), ("yl", "z")
MIB = 2**20


def swap(a, axis):
    return lax.ppermute(a, axis, [(0, 1), (1, 0)])


def bound_of(x):
    return jnp.ceil(jnp.log2(jnp.maximum(jnp.max(jnp.abs(x)), 2.0**-100)))


def enc(x, k):
    wide = jnp.pad(x, [(0, 0)] * (x.ndim - 2) + [(0, PAD), (0, 0)])
    row = lax.broadcasted_iota(jnp.int32, wide.shape, x.ndim - 2)
    return jnp.where(row < x.shape[-2], wide * jnp.exp2(TOP - k), k).astype(f16)


def dec(p):
    return p[..., :-PAD, :].astype(f32) * jnp.exp2(p[..., -1:, :].astype(f32) - TOP)


def gather_chips(a):
    return lax.all_to_all(jnp.broadcast_to(a, (16,) + a.shape), CHIPS, 0, 0, tiled=True)


def weave(own, other, c):
    first, second = jnp.where(c == 0, own, other), jnp.where(c == 0, other, own)
    return jnp.stack([first, second], axis=1).reshape((32,) + own.shape[1:])


def sum_row(keep, send):
    x = keep + swap(send, "c").astype(f32)
    blocks = enc(x, bound_of(x))
    return jnp.sum(dec(lax.all_to_all(blocks, CHIPS, 0, 0, tiled=True)), axis=0)


def sum_col(a):
    n, m = a.shape[0], a.shape[1] // 8
    blocks = enc(a.reshape(n, 8, m).transpose(1, 0, 2), bound_of(a))
    return jnp.sum(dec(lax.all_to_all(blocks, COL, 0, 0, tiled=True)), axis=0)


def shift_x(a, d):
    return lax.ppermute(a, "x", [(i, (i + d) % 4) for i in range(4)])


def place(where, parts):
    total = sum(p.shape[0] for p in parts)
    block = parts[0].shape[1:]

    def kernel(where_ref, *refs):
        out = refs[-1]
        n = 0
        for src in refs[:-1]:
            for j in range(src.shape[0]):
                out[where_ref[n]] = src[j]
                n += 1

    return pl.pallas_call(
        kernel,
        out_shape=jax.ShapeDtypeStruct((total,) + block, parts[0].dtype),
        in_specs=[pl.BlockSpec(memory_space=pltpu.SMEM)]
        + [pl.BlockSpec(memory_space=pltpu.VMEM)] * len(parts),
        out_specs=pl.BlockSpec(memory_space=pltpu.VMEM),
        compiler_params=pltpu.CompilerParams(vmem_limit_bytes=24 * MIB),
    )(where, *parts)


def gather_col(a, yh, x):
    p = enc(a, bound_of(a))
    two = jnp.stack([p, swap(p, "yh")])
    parts = [two] + [shift_x(two, d) for d in (1, -1, 2)]
    where = [(yh ^ j) * 4 + ((x - d) & 3) for d in (0, 1, -1, 2) for j in (0, 1)]
    blocks = place(jnp.stack(where).astype(jnp.int32), [dec(p) for p in parts])
    return blocks.transpose(1, 0, 2).reshape(a.shape[0], 8 * a.shape[1])


def weight_kernel(core_ref, tokens_ref, cotangent_ref, keep_ref, send_ref, total_ref):
    total_ref[...] = lax.dot_general(
        tokens_ref[...],
        cotangent_ref[...],
        (((0,), (0,)), ((), ())),
        preferred_element_type=f32,
    )
    core = core_ref[0]
    for j in range(2):
        keep_ref[j] = total_ref[pl.ds(pl.multiple_of(320 * j + 160 * core, 8), 160), :]
        send_ref[j] = total_ref[
            pl.ds(pl.multiple_of(320 * j + 160 * (1 - core), 8), 160), :
        ].astype(bf16)


def weight_parts(core, tokens, cotangent):
    return pl.pallas_call(
        weight_kernel,
        grid=(8,),
        in_specs=[
            pl.BlockSpec(memory_space=pltpu.SMEM),
            pl.BlockSpec((512, 640), lambda i: (0, i)),
            pl.BlockSpec((512, 384), lambda i: (0, 0)),
        ],
        out_specs=[pl.BlockSpec((2, 160, 384), lambda i: (i, 0, 0))] * 2,
        out_shape=[
            jax.ShapeDtypeStruct((16, 160, 384), f32),
            jax.ShapeDtypeStruct((16, 160, 384), bf16),
        ],
        scratch_shapes=[pltpu.VMEM((640, 384), f32)],
        compiler_params=pltpu.CompilerParams(vmem_limit_bytes=24 * MIB),
        cost_estimate=pl.CostEstimate(
            flops=2 * 512 * 5120 * 384, bytes_accessed=12 * MIB, transcendentals=0
        ),
    )(core[None], tokens, cotangent)


def shards(tokens, cotangent, teacher, expand_model, expand_heads):
    c, yh, x = lax.axis_index("c"), lax.axis_index("yh"), lax.axis_index("x")

    heads = lax.all_gather(expand_heads, ROW, axis=1, tiled=True)
    teacher_own = gather_chips(teacher)
    model_rows = gather_col(expand_model, yh, x)
    keep, send = weight_parts(c, tokens, cotangent)
    grad = sum_row(keep, send)

    teacher_block = weave(teacher_own, swap(teacher_own, "c"), c).reshape(4096, 256)
    expanded = jnp.dot(model_rows, teacher_block.astype(f32), precision=HIGH)
    expanded = gather_col(expanded, yh, x)
    student = lax.dot_general(expanded, heads, (((1,), (1,)), ((), ())), precision=HIGH)
    student = lax.all_gather(student.astype(bf16), ROW, axis=0, tiled=True)
    queries = jnp.dot(tokens, student, preferred_element_type=f32)

    share = lax.dot_general(
        expanded, grad, (((0,), (0,)), ((), ())), precision=HIGH, preferred_element_type=f32
    ).reshape(16, 2, 64, 384)
    keep = lax.dynamic_index_in_dim(share, c, 1, keepdims=False)
    send = lax.dynamic_index_in_dim(share, 1 - c, 1, keepdims=False).astype(bf16)
    grad_heads = sum_row(keep, send).T
    side = sum_col(jnp.dot(grad, heads, precision=HIGH))
    grad_model = sum_col(
        lax.dot_general(
            side, teacher_block.astype(f32), (((1,), (1,)), ((), ())), precision=HIGH
        )
    )
    return (queries, grad_model, grad_heads)


def solution(mesh):
    mesh = Mesh(mesh.devices.reshape(2, 8, 2, 2, 4), ROW + COL)
    in_specs = (P(ROW, None), P(ROW, COL), P(ROW, COL), P(ROW, COL), P(COL, ROW))
    out_specs = (P(ROW, COL), P(ROW, COL), P(COL, ROW))
    return jax.shard_map(
        shards, mesh=mesh, in_specs=in_specs, out_specs=out_specs, check_vma=False
    )
```

```python
import jax
import jax.numpy as jnp
from jax import lax
from jax.experimental import pallas as pl
from jax.experimental.pallas import tpu as pltpu
from jax.sharding import Mesh, PartitionSpec as P

f32, f16, bf16 = jnp.float32, jnp.float16, jnp.bfloat16
HIGH = lax.Precision.HIGH
PAD = 8
TOP = 14.0
ROW, COL, CHIPS = ("yl", "z", "c"), ("yh", "x"), ("yl", "z")
MIB = 2**20


def swap(a, axis):
    return lax.ppermute(a, axis, [(0, 1), (1, 0)])


def bound_of(x):
    return jnp.ceil(jnp.log2(jnp.maximum(jnp.max(jnp.abs(x)), 2.0**-100)))


def enc(x, k):
    wide = jnp.pad(x, [(0, 0)] * (x.ndim - 2) + [(0, PAD), (0, 0)])
    row = lax.broadcasted_iota(jnp.int32, wide.shape, x.ndim - 2)
    return jnp.where(row < x.shape[-2], wide * jnp.exp2(TOP - k), k).astype(f16)


def dec(p):
    return p[..., :-PAD, :].astype(f32) * jnp.exp2(p[..., -1:, :].astype(f32) - TOP)


def shift_z(a, d):
    pairs = [(i, (i // 2 + (d, -d)[i % 2]) % 8 * 2 + i % 2) for i in range(16)]
    return lax.ppermute(a, ("z", "c"), pairs)


def together(*arrays):
    return lax.optimization_barrier(arrays)


def chip_blocks(a, yl, c):
    mate = swap(a, "yl")
    two = jnp.stack([jnp.where(yl == 0, a, mate), jnp.where(yl == 0, mate, a)])
    mate = swap(two, "c")
    quad = jnp.stack([jnp.where(c == 0, two, mate), jnp.where(c == 0, mate, two)], axis=1)
    return quad.reshape((4,) + a.shape)


def far_blocks(quad, by2, c):
    by13 = shift_z(jnp.concatenate([quad, by2]), 1)
    by4 = shift_z(jnp.where(c == 0, by2[:2], by2[2:]), 2)
    return by13, by4


def gather_row(quad, mine, z, c):
    parts = [quad] + mine + [swap(p, "c") for p in mine]
    where = [i * 16 + z * 2 + j for i in (0, 1) for j in (0, 1)]
    for side in (1 - 2 * c, 2 * c - 1):
        for d in (2, 1, 3):
            where += [i * 16 + ((z - side * d) & 7) * 2 + j for i in (0, 1) for j in (0, 1)]
        where += [(1 - side) // 2 * 16 + ((z + 4) & 7) * 2 + j for j in (0, 1)]
    return place(jnp.stack(where).astype(jnp.int32), parts)


def blocks_row(keep, send, tops):
    n = keep.shape[1]
    got = swap(send, "c")
    top = tops[:, :1] + got[:, n : n + 1].astype(f32)
    k = jnp.ceil(jnp.log2(jnp.maximum(top, 2.0**-100)))
    return enc(keep + got[:, :n].astype(f32), k)


def swap_chips(blocks):
    return lax.all_to_all(blocks, CHIPS, 0, 0, tiled=True)


def swap_col(blocks):
    return lax.all_to_all(blocks, COL, 0, 0, tiled=True)


def col_blocks(a):
    n, m = a.shape[0], a.shape[1] // 8
    return enc(a.reshape(n, 8, m).transpose(1, 0, 2), bound_of(a))


def shift_x(a, d):
    return lax.ppermute(a, "x", [(i, (i + d) % 4) for i in range(4)])


def place(where, parts, columns=False):
    total = sum(p.shape[0] for p in parts)
    n, m = parts[0].shape[1:]

    def kernel(where_ref, *refs):
        out = refs[-1]
        i = 0
        for src in refs[:-1]:
            for j in range(src.shape[0]):
                if columns:
                    out[:, pl.ds(pl.multiple_of(where_ref[i] * m, 128), m)] = src[j]
                else:
                    out[where_ref[i]] = src[j]
                i += 1

    return pl.pallas_call(
        kernel,
        out_shape=jax.ShapeDtypeStruct((n, total * m) if columns else (total, n, m), parts[0].dtype),
        in_specs=[pl.BlockSpec(memory_space=pltpu.SMEM)]
        + [pl.BlockSpec(memory_space=pltpu.VMEM)] * len(parts),
        out_specs=pl.BlockSpec(memory_space=pltpu.VMEM),
        compiler_params=pltpu.CompilerParams(vmem_limit_bytes=24 * MIB),
    )(where, *parts)


def gather_col(a, yh, x, after=None):
    p = enc(a, bound_of(a))
    two = jnp.stack([p, swap(p, "yh")])
    if after is not None:
        two, after = lax.optimization_barrier((two, after))
    parts = [two] + [shift_x(two, d) for d in (1, -1, 2)]
    where = [(yh ^ j) * 4 + ((x - d) & 3) for d in (0, 1, -1, 2) for j in (0, 1)]
    out = place(jnp.stack(where).astype(jnp.int32), [dec(p) for p in parts], columns=True)
    return out if after is None else (out, after)


def split_cores(core, total_ref, j, n, keep_ref, send_ref, tops_ref):
    keep = total_ref[pl.ds(pl.multiple_of(2 * n * j + n * core, 8), n), :]
    send = total_ref[pl.ds(pl.multiple_of(2 * n * j + n * (1 - core), 8), n), :]
    m = keep.shape[1]
    keep_ref[j] = keep
    send_ref[j, :n] = send.astype(bf16)
    top = jnp.max(jnp.abs(send), axis=0, keepdims=True)
    send_ref[j, n:] = jnp.broadcast_to(top, (16, m)).astype(bf16)
    tops_ref[j] = jnp.broadcast_to(jnp.max(jnp.abs(keep), axis=0, keepdims=True), (8, m))


def weight_kernel(core_ref, tokens_ref, cotangent_ref, keep_ref, send_ref, tops_ref, total_ref):
    total_ref[...] = lax.dot_general(
        tokens_ref[...],
        cotangent_ref[...],
        (((0,), (0,)), ((), ())),
        preferred_element_type=f32,
    )
    for j in range(2):
        split_cores(core_ref[0], total_ref, j, 160, keep_ref, send_ref, tops_ref)


def split_shapes(n):
    return [
        jax.ShapeDtypeStruct((16, n, 384), f32),
        jax.ShapeDtypeStruct((16, n + 16, 384), bf16),
        jax.ShapeDtypeStruct((16, 8, 384), f32),
    ]


def weight_parts(core, tokens, cotangent):
    return pl.pallas_call(
        weight_kernel,
        grid=(8,),
        in_specs=[
            pl.BlockSpec(memory_space=pltpu.SMEM),
            pl.BlockSpec((512, 640), lambda i: (0, i)),
            pl.BlockSpec((512, 384), lambda i: (0, 0)),
        ],
        out_specs=[pl.BlockSpec((2,) + s.shape[1:], lambda i: (i, 0, 0)) for s in split_shapes(160)],
        out_shape=split_shapes(160),
        scratch_shapes=[pltpu.VMEM((640, 384), f32)],
        compiler_params=pltpu.CompilerParams(vmem_limit_bytes=24 * MIB),
        cost_estimate=pl.CostEstimate(
            flops=2 * 512 * 5120 * 384, bytes_accessed=12 * MIB, transcendentals=0
        ),
    )(core[None], tokens, cotangent)


def halves(a):
    high = a.astype(bf16)
    return high, (a - high.astype(f32)).astype(bf16)


def share_kernel(core_ref, expanded_ref, grad_ref, keep_ref, send_ref, tops_ref, total_ref):
    grad_hi, grad_lo = halves(grad_ref[...])

    def product(a, b):
        return lax.dot_general(a, b, (((0,), (0,)), ((), ())), preferred_element_type=f32)

    for i in range(4):
        hi, lo = halves(expanded_ref[:, 512 * i : 512 * i + 512])
        total_ref[512 * i : 512 * i + 512] = (
            product(hi, grad_hi) + product(hi, grad_lo) + product(lo, grad_hi)
        )
    for j in range(16):
        split_cores(core_ref[0], total_ref, j, 64, keep_ref, send_ref, tops_ref)


def share_parts(core, expanded, grad):
    return pl.pallas_call(
        share_kernel,
        in_specs=[pl.BlockSpec(memory_space=pltpu.SMEM)] + [pl.BlockSpec(memory_space=pltpu.VMEM)] * 2,
        out_specs=[pl.BlockSpec(memory_space=pltpu.VMEM)] * 3,
        out_shape=split_shapes(64),
        scratch_shapes=[pltpu.VMEM((2048, 384), f32)],
        compiler_params=pltpu.CompilerParams(vmem_limit_bytes=24 * MIB),
        cost_estimate=pl.CostEstimate(
            flops=6 * 160 * 2048 * 384, bytes_accessed=6 * MIB, transcendentals=0
        ),
    )(core[None], expanded, grad)


def shards(tokens, cotangent, teacher, expand_model, expand_heads):
    yl, z, c = [lax.axis_index(name) for name in ROW]
    yh, x = [lax.axis_index(name) for name in COL]

    heads = lax.all_gather(expand_heads, ROW, axis=1, tiled=True)
    teacher_quad = chip_blocks(teacher, yl, c)
    teacher_by2 = shift_z(teacher_quad, 2)
    blocks = blocks_row(*weight_parts(c, tokens, cotangent))
    blocks, teacher_by2 = together(blocks, teacher_by2)
    model_rows, blocks = gather_col(expand_model, yh, x, blocks)
    grad = jnp.sum(dec(swap_chips(blocks)), axis=0)

    mine = [teacher_by2, *far_blocks(teacher_quad, teacher_by2, c)]
    teacher_block = gather_row(teacher_quad, mine, z, c).reshape(4096, 256)
    expanded = jnp.dot(model_rows, teacher_block.astype(f32), precision=HIGH)
    expanded = gather_col(expanded, yh, x)
    student = lax.dot_general(expanded, heads, (((1,), (1,)), ((), ())), precision=HIGH)
    student_quad = chip_blocks(student.astype(bf16), yl, c)
    student_by2 = shift_z(student_quad, 2)

    side = swap_col(col_blocks(jnp.dot(grad, heads, precision=HIGH)))
    side, student_by2 = together(side, student_by2)
    student_by13, student_by4 = far_blocks(student_quad, student_by2, c)
    grad_heads = swap_chips(blocks_row(*share_parts(c, expanded, grad)))
    side = jnp.sum(dec(side), axis=0)
    blocks = col_blocks(
        lax.dot_general(
            side, teacher_block.astype(f32), (((1,), (1,)), ((), ())), precision=HIGH
        )
    )
    blocks, grad_heads, student_by13, student_by4 = together(
        blocks, grad_heads, student_by13, student_by4
    )
    grad_model = jnp.sum(dec(swap_col(blocks)), axis=0)
    grad_heads = jnp.sum(dec(grad_heads), axis=0).T

    mine = [student_by2, student_by13, student_by4]
    student = gather_row(student_quad, mine, z, c).reshape(5120, 384)
    queries = jnp.dot(tokens, student, preferred_element_type=f32)
    return (queries, grad_model, grad_heads)


def solution(mesh):
    mesh = Mesh(mesh.devices.reshape(2, 8, 2, 2, 4), ROW + COL)
    in_specs = (P(ROW, None), P(ROW, COL), P(ROW, COL), P(ROW, COL), P(COL, ROW))
    out_specs = (P(ROW, COL), P(ROW, COL), P(COL, ROW))
    return jax.shard_map(
        shards, mesh=mesh, in_specs=in_specs, out_specs=out_specs, check_vma=False
    )
```

```python
import jax
import jax.numpy as jnp
from jax import lax
from jax.experimental import pallas as pl
from jax.experimental.pallas import tpu as pltpu
from jax.sharding import Mesh, PartitionSpec as P

f32, f16, bf16 = jnp.float32, jnp.float16, jnp.bfloat16
HIGH = lax.Precision.HIGH
PAD = 8
TOP = 14.0
ROW, COL, CHIPS = ("yl", "z", "c"), ("yh", "x"), ("yl", "z")
MIB = 2**20


def swap(a, axis):
    return lax.ppermute(a, axis, [(0, 1), (1, 0)])


def bound_of(x):
    return jnp.ceil(jnp.log2(jnp.maximum(jnp.max(jnp.abs(x)), 2.0**-100)))


def enc(x, k):
    wide = jnp.pad(x, [(0, 0)] * (x.ndim - 2) + [(0, PAD), (0, 0)])
    row = lax.broadcasted_iota(jnp.int32, wide.shape, x.ndim - 2)
    return jnp.where(row < x.shape[-2], wide * jnp.exp2(TOP - k), k).astype(f16)


def dec(p):
    return p[..., :-PAD, :].astype(f32) * jnp.exp2(p[..., -1:, :].astype(f32) - TOP)


def shift_z(a, d):
    pairs = [(i, (i // 2 + (d, -d)[i % 2]) % 8 * 2 + i % 2) for i in range(16)]
    return lax.ppermute(a, ("z", "c"), pairs)


def after(a, *others):
    return lax.optimization_barrier((a, *others))[0]


def chip_blocks(a, yl, c):
    mate = swap(a, "yl")
    two = jnp.stack([jnp.where(yl == 0, a, mate), jnp.where(yl == 0, mate, a)])
    mate = swap(two, "c")
    quad = jnp.stack([jnp.where(c == 0, two, mate), jnp.where(c == 0, mate, two)], axis=1)
    return quad.reshape((4,) + a.shape)


def far_blocks(quad, by2, c):
    by13 = shift_z(jnp.concatenate([quad, by2]), 1)
    by4 = shift_z(jnp.where(c == 0, by2[:2], by2[2:]), 2)
    return by13, by4


def gather_row(quad, mine, z, c):
    parts = [quad] + mine + [swap(p, "c") for p in mine]
    where = [i * 16 + z * 2 + j for i in (0, 1) for j in (0, 1)]
    for side in (1 - 2 * c, 2 * c - 1):
        for d in (2, 1, 3):
            where += [i * 16 + ((z - side * d) & 7) * 2 + j for i in (0, 1) for j in (0, 1)]
        where += [(1 - side) // 2 * 16 + ((z + 4) & 7) * 2 + j for j in (0, 1)]
    return place(jnp.stack(where).astype(jnp.int32), parts)


def halves_row(keep, send, tops, yl):
    n, m = keep.shape[1:]
    got = swap(send, "c").reshape(2, 8, n + 16, m)
    keep, tops = keep.reshape(2, 8, n, m), tops.reshape(2, 8, 8, m)

    def half(i):
        a, b, t = [lax.dynamic_index_in_dim(v, i, 0, keepdims=False) for v in (keep, got, tops)]
        return a + b[:, :n].astype(f32), t[:, :1] + b[:, n : n + 1].astype(f32)

    x, top = half(1 - yl)
    return enc(x, scale_of(top)), half(yl)


def scale_of(top):
    return jnp.ceil(jnp.log2(jnp.maximum(top, 2.0**-100)))


def blocks_z(payload, half):
    mate = swap(payload, "yl")
    x, top = half
    return enc(x + dec(mate), scale_of(top + jnp.exp2(mate[:, -1:].astype(f32))))


def sum_z(blocks, z):
    total = dec(lax.dynamic_index_in_dim(blocks, z, 0, keepdims=False))
    for d in range(1, 8):
        block = lax.dynamic_index_in_dim(blocks, (z + d) & 7, 0, keepdims=False)
        total += dec(lax.ppermute(block, "z", [(i, (i + d) % 8) for i in range(8)]))
    return total


def copies(a):
    return jnp.broadcast_to(a, (16,) + a.shape)


def gather_chips(blocks):
    return lax.all_to_all(blocks, CHIPS, 0, 0, tiled=True)


def weave(own, c):
    other = swap(own, "c")
    first, second = jnp.where(c == 0, own, other), jnp.where(c == 0, other, own)
    return jnp.stack([first, second], axis=1).reshape((32,) + own.shape[1:])


def swap_col(blocks):
    return lax.all_to_all(blocks, COL, 0, 0, tiled=True)


def col_blocks(a):
    n, m = a.shape[0], a.shape[1] // 8
    return enc(a.reshape(n, 8, m).transpose(1, 0, 2), bound_of(a))


def shift_x(a, d):
    return lax.ppermute(a, "x", [(i, (i + d) % 4) for i in range(4)])


def place(where, parts, columns=False):
    total = sum(p.shape[0] for p in parts)
    n, m = parts[0].shape[1:]

    def kernel(where_ref, *refs):
        out = refs[-1]
        i = 0
        for src in refs[:-1]:
            for j in range(src.shape[0]):
                if columns:
                    out[:, pl.ds(pl.multiple_of(where_ref[i] * m, 128), m)] = src[j]
                else:
                    out[where_ref[i]] = src[j]
                i += 1

    return pl.pallas_call(
        kernel,
        out_shape=jax.ShapeDtypeStruct((n, total * m) if columns else (total, n, m), parts[0].dtype),
        in_specs=[pl.BlockSpec(memory_space=pltpu.SMEM)]
        + [pl.BlockSpec(memory_space=pltpu.VMEM)] * len(parts),
        out_specs=pl.BlockSpec(memory_space=pltpu.VMEM),
        compiler_params=pltpu.CompilerParams(vmem_limit_bytes=24 * MIB),
    )(where, *parts)


def pair_col(a):
    p = enc(a, bound_of(a))
    return jnp.stack([p, swap(p, "yh")])


def gather_col(two, yh, x):
    parts = [two] + [shift_x(two, d) for d in (1, -1, 2)]
    where = [(yh ^ j) * 4 + ((x - d) & 3) for d in (0, 1, -1, 2) for j in (0, 1)]
    return place(jnp.stack(where).astype(jnp.int32), [dec(p) for p in parts], columns=True)


def split_cores(core, total_ref, j, n, keep_ref, send_ref, tops_ref):
    keep = total_ref[pl.ds(pl.multiple_of(2 * n * j + n * core, 8), n), :]
    send = total_ref[pl.ds(pl.multiple_of(2 * n * j + n * (1 - core), 8), n), :]
    m = keep.shape[1]
    keep_ref[j] = keep
    send_ref[j, :n] = send.astype(bf16)
    top = jnp.max(jnp.abs(send), axis=0, keepdims=True)
    send_ref[j, n:] = jnp.broadcast_to(top, (16, m)).astype(bf16)
    tops_ref[j] = jnp.broadcast_to(jnp.max(jnp.abs(keep), axis=0, keepdims=True), (8, m))


def weight_kernel(core_ref, tokens_ref, cotangent_ref, keep_ref, send_ref, tops_ref, total_ref):
    total_ref[...] = lax.dot_general(
        tokens_ref[...],
        cotangent_ref[...],
        (((0,), (0,)), ((), ())),
        preferred_element_type=f32,
    )
    for j in range(2):
        split_cores(core_ref[0], total_ref, j, 160, keep_ref, send_ref, tops_ref)


def split_shapes(n):
    return [
        jax.ShapeDtypeStruct((16, n, 384), f32),
        jax.ShapeDtypeStruct((16, n + 16, 384), bf16),
        jax.ShapeDtypeStruct((16, 8, 384), f32),
    ]


def weight_parts(core, tokens, cotangent):
    return pl.pallas_call(
        weight_kernel,
        grid=(8,),
        in_specs=[
            pl.BlockSpec(memory_space=pltpu.SMEM),
            pl.BlockSpec((512, 640), lambda i: (0, i)),
            pl.BlockSpec((512, 384), lambda i: (0, 0)),
        ],
        out_specs=[pl.BlockSpec((2,) + s.shape[1:], lambda i: (i, 0, 0)) for s in split_shapes(160)],
        out_shape=split_shapes(160),
        scratch_shapes=[pltpu.VMEM((640, 384), f32)],
        compiler_params=pltpu.CompilerParams(vmem_limit_bytes=24 * MIB),
        cost_estimate=pl.CostEstimate(
            flops=2 * 512 * 5120 * 384, bytes_accessed=12 * MIB, transcendentals=0
        ),
    )(core[None], tokens, cotangent)


def halves(a):
    high = a.astype(bf16)
    return high, (a - high.astype(f32)).astype(bf16)


def share_kernel(core_ref, expanded_ref, grad_ref, keep_ref, send_ref, tops_ref, total_ref):
    grad_hi, grad_lo = halves(grad_ref[...])

    def product(a, b):
        return lax.dot_general(a, b, (((0,), (0,)), ((), ())), preferred_element_type=f32)

    for i in range(4):
        hi, lo = halves(expanded_ref[:, 512 * i : 512 * i + 512])
        total_ref[512 * i : 512 * i + 512] = (
            product(hi, grad_hi) + product(hi, grad_lo) + product(lo, grad_hi)
        )
    for j in range(16):
        split_cores(core_ref[0], total_ref, j, 64, keep_ref, send_ref, tops_ref)


def share_parts(core, expanded, grad):
    return pl.pallas_call(
        share_kernel,
        in_specs=[pl.BlockSpec(memory_space=pltpu.SMEM)] + [pl.BlockSpec(memory_space=pltpu.VMEM)] * 2,
        out_specs=[pl.BlockSpec(memory_space=pltpu.VMEM)] * 3,
        out_shape=split_shapes(64),
        scratch_shapes=[pltpu.VMEM((2048, 384), f32)],
        compiler_params=pltpu.CompilerParams(vmem_limit_bytes=24 * MIB),
        cost_estimate=pl.CostEstimate(
            flops=6 * 160 * 2048 * 384, bytes_accessed=6 * MIB, transcendentals=0
        ),
    )(core[None], expanded, grad)


def shards(tokens, cotangent, teacher, expand_model, expand_heads):
    yl, z, c = [lax.axis_index(name) for name in ROW]
    yh, x = [lax.axis_index(name) for name in COL]

    payload, half = halves_row(*weight_parts(c, tokens, cotangent), yl)
    wide, heads_t = teacher.astype(f32), expand_heads.T
    tail = jnp.concatenate([heads_t[:32, 256:], heads_t[32:, 256:]], axis=1)
    packed = jnp.concatenate([heads_t[:, :256], tail])
    both = jnp.concatenate([enc(wide, bound_of(wide)), enc(packed, bound_of(packed))])
    both = weave(after(gather_chips(copies(both)), payload), c)
    teacher_block = dec(both[:, : 128 + PAD]).astype(bf16).reshape(4096, 256)
    packed = dec(both[:, 128 + PAD :])
    tail = jnp.concatenate([packed[:, 64:, :128], packed[:, 64:, 128:]], axis=1)
    heads = jnp.concatenate([packed[:, :64], tail], axis=2).reshape(2048, 384)
    blocks = blocks_z(payload, half)

    model_rows = gather_col(after(pair_col(expand_model), payload), yh, x)
    expanded = jnp.dot(model_rows, teacher_block.astype(f32), precision=HIGH)
    expanded_two = pair_col(expanded)
    expanded = gather_col(expanded_two, yh, x)
    blocks = after(lax.all_to_all(blocks, "z", 0, 0, tiled=True), expanded)
    grad = jnp.sum(dec(blocks), axis=0)
    student_quad = chip_blocks(jnp.dot(expanded, heads, precision=HIGH).astype(bf16), yl, c)
    student_by2 = shift_z(student_quad, 2)

    side = swap_col(
        col_blocks(lax.dot_general(grad, heads, (((1,), (1,)), ((), ())), precision=HIGH))
    )
    student_by13, student_by4 = far_blocks(student_quad, student_by2, c)
    side = jnp.sum(dec(after(side, student_by2)), axis=0)
    blocks = col_blocks(
        lax.dot_general(
            side, teacher_block.astype(f32), (((1,), (1,)), ((), ())), precision=HIGH
        )
    )
    grad_model = jnp.sum(dec(swap_col(blocks)), axis=0)
    payload, half = halves_row(*share_parts(c, expanded, grad), yl)
    grad_heads = sum_z(after(blocks_z(payload, half), blocks), z).T

    mine = [student_by2, student_by13, student_by4]
    student = gather_row(student_quad, mine, z, c).reshape(5120, 384)
    queries = jnp.dot(tokens, student, preferred_element_type=f32)
    return (queries, grad_model, grad_heads)


def solution(mesh):
    mesh = Mesh(mesh.devices.reshape(2, 8, 2, 2, 4), ROW + COL)
    in_specs = (P(ROW, None), P(ROW, COL), P(ROW, COL), P(ROW, COL), P(COL, ROW))
    out_specs = (P(ROW, COL), P(ROW, COL), P(COL, ROW))
    return jax.shard_map(
        shards, mesh=mesh, in_specs=in_specs, out_specs=out_specs, check_vma=False
    )
```

```python
import jax
import jax.numpy as jnp
from jax import lax
from jax.experimental import pallas as pl
from jax.experimental.pallas import tpu as pltpu
from jax.sharding import Mesh, PartitionSpec as P

f32, f16, bf16 = jnp.float32, jnp.float16, jnp.bfloat16
HIGH = lax.Precision.HIGH
PAD = 16
TOP = 14.0
ROW, COL = ("yl", "z", "c"), ("yh", "x")
MIB = 2**20
VMEM, SMEM = pl.BlockSpec(memory_space=pltpu.VMEM), pl.BlockSpec(memory_space=pltpu.SMEM)


def swap(a, axis):
    return lax.ppermute(a, axis, [(0, 1), (1, 0)])


def after(a, *others):
    return lax.optimization_barrier((a, *others))[0]


def scale_of(top):
    return jnp.ceil(jnp.log2(jnp.maximum(top, 2.0**-100)))


def rows_of(a):
    return lax.broadcasted_iota(jnp.int32, a.shape, a.ndim - 2)


def payload(a):
    n = a.shape[-2] - PAD
    k = scale_of(a[..., n : n + 1, :])
    return jnp.where(rows_of(a) < n, a * jnp.exp2(TOP - k), k).astype(f16)


def dec(p):
    return p[..., :-PAD, :].astype(f32) * jnp.exp2(p[..., -1:, :].astype(f32) - TOP)


def enc(a):
    wide = jnp.pad(a, [(0, PAD), (0, 0)])
    k = scale_of(jnp.max(jnp.abs(a)))
    return jnp.where(rows_of(wide) < a.shape[0], wide * jnp.exp2(TOP - k), k).astype(f16)


def halves(a):
    high = a.astype(bf16)
    return high, (a - high.astype(f32)).astype(bf16)


def pair_y(a, yl):
    mate = swap(a, "yl")
    return jnp.stack([jnp.where(yl == 0, a, mate), jnp.where(yl == 0, mate, a)])


def gather_z(two):
    return lax.all_gather(two, "z").reshape((16,) + two.shape[1:])


def place(where, parts, columns=False, join=False):
    total = sum(p.shape[0] for p in parts)
    n, m = parts[0].shape[1:]
    kind = parts[0].dtype
    if join:
        n, kind = n // 2, f32

    def kernel(where_ref, *refs):
        out = refs[-1]
        i = 0
        for src in refs[:-1]:
            for j in range(src.shape[0]):
                if columns:
                    out[:, pl.ds(pl.multiple_of(where_ref[i] * m, 128), m)] = src[j]
                elif join:
                    out[where_ref[i]] = src[j, :n].astype(f32) + src[j, n:].astype(f32)
                else:
                    out[where_ref[i]] = src[j]
                i += 1

    return pl.pallas_call(
        kernel,
        out_shape=jax.ShapeDtypeStruct((n, total * m) if columns else (total, n, m), kind),
        in_specs=[SMEM] + [VMEM] * len(parts),
        out_specs=VMEM,
        compiler_params=pltpu.CompilerParams(vmem_limit_bytes=24 * MIB),
    )(where, *parts)


def weave(own, c, join=False):
    where = [i * 16 + z * 2 + k for k in (c, 1 - c) for z in range(8) for i in (0, 1)]
    return place(jnp.stack(where).astype(jnp.int32), [own, swap(own, "c")], join=join)


def pair_col(a):
    p = enc(a)
    return jnp.stack([p, swap(p, "yh")])


def gather_col(two, yh, x):
    parts = [two]
    parts += [lax.ppermute(two, "x", [(i, (i + d) % 4) for i in range(4)]) for d in (1, -1, 2)]
    where = [(yh ^ j) * 4 + ((x - d) & 3) for d in (0, 1, -1, 2) for j in (0, 1)]
    return place(jnp.stack(where).astype(jnp.int32), [dec(p) for p in parts], columns=True)


def swap_col(blocks):
    return lax.all_to_all(blocks, COL, 0, 0, tiled=True)


def sum_mates(keep, send):
    x = keep + swap(send, "c").astype(f32)
    return payload(x[1]), x[0]


def blocks_z(sent, own):
    mate = swap(sent, "yl")
    n = own.shape[1] - PAD
    k = mate[:, n : n + 1].astype(f32)
    got = jnp.where(rows_of(own) < n, mate.astype(f32) * jnp.exp2(k - TOP), jnp.exp2(k))
    return payload(own + got)


def parts_z(blocks, z):
    got = [lax.dynamic_index_in_dim(blocks, z, 0, keepdims=False)]
    for d in range(1, 8):
        block = lax.dynamic_index_in_dim(blocks, (z + d) & 7, 0, keepdims=False)
        got.append(lax.ppermute(block, "z", [(i, (i + d) % 8) for i in range(8)]))
    return got


def with_top(a, rows):
    return jnp.broadcast_to(jnp.max(jnp.abs(a), axis=0, keepdims=True), (rows, a.shape[1]))


def split_cores(core, total_ref, j, n, keep_ref, send_ref, at):
    keep = total_ref[pl.ds(pl.multiple_of(2 * n * j + n * core, 8), n), :]
    send = total_ref[pl.ds(pl.multiple_of(2 * n * j + n * (1 - core), 8), n), :]
    keep_ref[(*at, slice(0, n))] = keep
    keep_ref[(*at, slice(n, n + PAD))] = with_top(keep, PAD)
    send_ref[(*at, slice(0, n))] = send.astype(bf16)
    send_ref[(*at, slice(n, n + PAD))] = with_top(send, PAD).astype(bf16)


def weight_kernel(place_ref, tokens_ref, cotangent_ref, keep_ref, send_ref, total_ref):
    total_ref[...] = lax.dot_general(
        tokens_ref[...],
        cotangent_ref[...],
        (((0,), (0,)), ((), ())),
        preferred_element_type=f32,
    )
    for j in range(2):
        split_cores(place_ref[1], total_ref, j, 160, keep_ref, send_ref, (0, j))


def split_shapes(n):
    return [jax.ShapeDtypeStruct((2, 8, n + PAD, 384), kind) for kind in (f32, bf16)]


def weight_parts(yl, c, tokens, cotangent):
    block = pl.BlockSpec((1, 2, 160 + PAD, 384), lambda i, where: (where[0] ^ (i // 4), i % 4, 0, 0))
    return pl.pallas_call(
        weight_kernel,
        grid_spec=pltpu.PrefetchScalarGridSpec(
            num_scalar_prefetch=1,
            grid=(8,),
            in_specs=[
                pl.BlockSpec((512, 640), lambda i, where: (0, i)),
                pl.BlockSpec((512, 384), lambda i, where: (0, 0)),
            ],
            out_specs=[block, block],
            scratch_shapes=[pltpu.VMEM((640, 384), f32)],
        ),
        out_shape=split_shapes(160),
        compiler_params=pltpu.CompilerParams(vmem_limit_bytes=24 * MIB),
        cost_estimate=pl.CostEstimate(
            flops=2 * 512 * 5120 * 384, bytes_accessed=12 * MIB, transcendentals=0
        ),
    )(jnp.stack([yl, c]).astype(jnp.int32), tokens, cotangent)


def product(a, b, contract):
    return sum(
        lax.dot_general(u, v, (contract, ((), ())), preferred_element_type=f32)
        for u, v in ((a[0], b[0]), (a[0], b[1]), (a[1], b[0]))
    )


def share_kernel(place_ref, expanded_ref, grad_ref, keep_ref, send_ref, total_ref):
    grad = halves(grad_ref[...])
    for i in range(4):
        rows = slice(512 * i, 512 * i + 512)
        total_ref[rows] = product(halves(expanded_ref[:, rows]), grad, ((0,), (0,)))
    for j in range(16):
        split_cores(
            place_ref[1], total_ref, j, 64, keep_ref, send_ref, (place_ref[0] ^ (j // 8), j % 8)
        )


def share_parts(yl, c, expanded, grad):
    return pl.pallas_call(
        share_kernel,
        in_specs=[SMEM, VMEM, VMEM],
        out_specs=[VMEM, VMEM],
        out_shape=split_shapes(64),
        scratch_shapes=[pltpu.VMEM((2048, 384), f32)],
        compiler_params=pltpu.CompilerParams(vmem_limit_bytes=24 * MIB),
        cost_estimate=pl.CostEstimate(
            flops=6 * 160 * 2048 * 384, bytes_accessed=6 * MIB, transcendentals=0
        ),
    )(jnp.stack([yl, c]).astype(jnp.int32), expanded, grad)


def blocks_kernel(a_ref, b_ref, out_ref):
    a = halves(a_ref[...])
    n, m = a[0].shape[0], out_ref.shape[2]
    for q in range(8):
        b = b_ref[q * m : q * m + m, :]
        if b.dtype == bf16:
            total = sum(
                lax.dot_general(u, b, (((1,), (1,)), ((), ())), preferred_element_type=f32) for u in a
            )
        else:
            total = product(a, halves(b), ((1,), (1,)))
        out_ref[q, :n] = total
        out_ref[q, n:] = with_top(total, PAD)


def blocks_of(a, b):
    n, m = a.shape[0], b.shape[0] // 8
    return pl.pallas_call(
        blocks_kernel,
        in_specs=[VMEM, VMEM],
        out_specs=VMEM,
        out_shape=jax.ShapeDtypeStruct((8, n + PAD, m), f32),
        compiler_params=pltpu.CompilerParams(vmem_limit_bytes=24 * MIB),
        cost_estimate=pl.CostEstimate(
            flops=6 * a.shape[0] * b.size, bytes_accessed=6 * MIB, transcendentals=0
        ),
    )(a, b)


def shards(tokens, cotangent, teacher, expand_model, expand_heads):
    yl, z, c = [lax.axis_index(name) for name in ROW]
    yh, x = [lax.axis_index(name) for name in COL]

    sent, own = sum_mates(*weight_parts(yl, c, tokens, cotangent))
    teacher_own = after(gather_z(pair_y(teacher, yl)), sent)
    model_two = after(pair_col(expand_model), sent)
    heads_two = pair_y(jnp.concatenate(halves(expand_heads.T)), yl)
    heads_own = gather_z(after(heads_two, teacher_own))

    teacher_block = weave(teacher_own, c).reshape(4096, 256)
    model_rows = gather_col(model_two, yh, x)
    expanded_two = pair_col(jnp.dot(model_rows, teacher_block.astype(f32), precision=HIGH))
    expanded = gather_col(expanded_two, yh, x)
    blocks = lax.all_to_all(blocks_z(sent, own), "z", 0, 0, tiled=True)
    grad = jnp.sum(dec(after(blocks, expanded)), axis=0)

    heads = weave(heads_own, c, join=True).reshape(2048, 384)
    student = jnp.dot(expanded, heads, precision=HIGH).astype(bf16)
    student_own = gather_z(pair_y(student, yl))

    side = jnp.sum(dec(swap_col(payload(blocks_of(grad, heads)))), axis=0)
    blocks = payload(blocks_of(side, teacher_block))
    grad_model = jnp.sum(dec(swap_col(blocks)), axis=0)
    shares = blocks_z(*sum_mates(*share_parts(yl, c, expanded, grad)))
    shares = parts_z(after(shares, blocks), z)
    grad_heads = sum(dec(p) for p in shares).T

    student = weave(after(student_own, blocks), c).reshape(5120, 384)
    queries = jnp.dot(tokens, student, preferred_element_type=f32)
    return (queries, grad_model, grad_heads)


def solution(mesh):
    mesh = Mesh(mesh.devices.reshape(2, 8, 2, 2, 4), ROW + COL)
    in_specs = (P(ROW, None), P(ROW, COL), P(ROW, COL), P(ROW, COL), P(COL, ROW))
    out_specs = (P(ROW, COL), P(ROW, COL), P(COL, ROW))
    return jax.shard_map(
        shards, mesh=mesh, in_specs=in_specs, out_specs=out_specs, check_vma=False
    )
```

```python
import jax
import jax.numpy as jnp
from jax import lax
from jax.experimental import pallas as pl
from jax.experimental.pallas import tpu as pltpu
from jax.sharding import Mesh, PartitionSpec as P

f32, f16, bf16 = jnp.float32, jnp.float16, jnp.bfloat16
HIGH = lax.Precision.HIGH
PAD = 16
TOP = 14.0
ROW, COL = ("yl", "z", "c"), ("yh", "x")
MIB = 2**20
VMEM, SMEM = pl.BlockSpec(memory_space=pltpu.VMEM), pl.BlockSpec(memory_space=pltpu.SMEM)


def swap(a, axis):
    return lax.ppermute(a, axis, [(0, 1), (1, 0)])


def after(a, *others):
    return lax.optimization_barrier((a, *others))[0]


def scale_of(top):
    return jnp.ceil(jnp.log2(jnp.maximum(top, 2.0**-100)))


def rows_of(a):
    return lax.broadcasted_iota(jnp.int32, a.shape, a.ndim - 2)


def payload(a):
    n = a.shape[-2] - PAD
    k = scale_of(a[..., n : n + 1, :])
    return jnp.where(rows_of(a) < n, a * jnp.exp2(TOP - k), k).astype(f16)


def dec(p):
    return p[..., :-PAD, :].astype(f32) * jnp.exp2(p[..., -1:, :].astype(f32) - TOP)


def enc(a):
    wide = jnp.pad(a, [(0, PAD), (0, 0)])
    k = scale_of(jnp.max(jnp.abs(a)))
    return jnp.where(rows_of(wide) < a.shape[0], wide * jnp.exp2(TOP - k), k).astype(f16)


def halves(a):
    high = a.astype(bf16)
    return high, (a - high.astype(f32)).astype(bf16)


def halves_outside(a):
    high = lax.reduce_precision(a, 8, 7)
    return high.astype(bf16), (a - high).astype(bf16)


def pair_y(a, yl):
    mate = swap(a, "yl")
    return jnp.stack([jnp.where(yl == 0, a, mate), jnp.where(yl == 0, mate, a)])


def gather_z(two):
    return lax.all_gather(two, "z").reshape((16,) + two.shape[1:])


def place(where, parts, shape, put):
    def kernel(where_ref, *refs):
        i = 0
        for src in refs[: len(parts)]:
            for j in range(src.shape[0]):
                put(refs[len(parts) :], where_ref[i], src[j])
                i += 1

    return pl.pallas_call(
        kernel,
        out_shape=shape,
        in_specs=[SMEM] + [VMEM] * len(parts),
        out_specs=jax.tree.map(lambda _: VMEM, shape),
        compiler_params=pltpu.CompilerParams(vmem_limit_bytes=24 * MIB),
    )(jnp.stack(where).astype(jnp.int32), *parts)


def put_rows(outs, at, block):
    outs[0][at] = block


def put_columns(outs, at, block):
    m = block.shape[1]
    outs[0][:, pl.ds(pl.multiple_of(at * m, 128), m)] = block


def put_teacher_heads(outs, at, block):
    teacher, heads = outs
    teacher[at] = block[:128]
    both = block[128:224].astype(f32) + block[224:].astype(f32)
    heads[at, :, :256] = both[:64]
    heads[at, :32, 256:] = both[64:, :128]
    heads[at, 32:, 256:] = both[64:, 128:]


def pack_teacher_heads(teacher, heads_t):
    rows = [teacher]
    for half in halves_outside(heads_t):
        rows += [half[:, :256], jnp.concatenate([half[:32, 256:], half[32:, 256:]], axis=1)]
    return jnp.concatenate(rows)


def weave(own, c, shape, put, pieces=1):
    where = [i * 16 + z * 2 + k for k in (c, 1 - c) for z in range(8) for i in (0, 1)]
    mine = jnp.split(own, pieces)
    return place(where, mine + [swap(p, "c") for p in mine], shape, put)


def pair_col(a):
    p = enc(a)
    return jnp.stack([p, swap(p, "yh")])


def gather_col(two, yh, x):
    parts = [two]
    parts += [lax.ppermute(two, "x", [(i, (i + d) % 4) for i in range(4)]) for d in (1, -1, 2)]
    where = [(yh ^ j) * 4 + ((x - d) & 3) for d in (0, 1, -1, 2) for j in (0, 1)]
    n, m = two.shape[1] - PAD, two.shape[2]
    shape = jax.ShapeDtypeStruct((n, 8 * m), f32)
    return place(where, [dec(p) for p in parts], shape, put_columns)


def swap_col(blocks):
    return lax.all_to_all(blocks, COL, 0, 0, tiled=True)


def sum_mates(keep, send):
    x = keep + swap(send, "c").astype(f32)
    return payload(x[1]), x[0]


def blocks_z(sent, own):
    mate = swap(sent, "yl")
    n = own.shape[1] - PAD
    k = mate[:, n : n + 1].astype(f32)
    got = jnp.where(rows_of(own) < n, mate.astype(f32) * jnp.exp2(k - TOP), jnp.exp2(k))
    return payload(own + got)


def parts_z(blocks, z):
    got = [lax.dynamic_index_in_dim(blocks, z, 0, keepdims=False)]
    for d in range(1, 8):
        block = lax.dynamic_index_in_dim(blocks, (z + d) & 7, 0, keepdims=False)
        got.append(lax.ppermute(block, "z", [(i, (i + d) % 8) for i in range(8)]))
    return got


def with_top(a, rows):
    return jnp.broadcast_to(jnp.max(jnp.abs(a), axis=0, keepdims=True), (rows, a.shape[1]))


def split_cores(core, total_ref, j, n, keep_ref, send_ref, at):
    keep = total_ref[pl.ds(pl.multiple_of(2 * n * j + n * core, 8), n), :]
    send = total_ref[pl.ds(pl.multiple_of(2 * n * j + n * (1 - core), 8), n), :]
    keep_ref[(*at, slice(0, n))] = keep
    keep_ref[(*at, slice(n, n + PAD))] = with_top(keep, PAD)
    send_ref[(*at, slice(0, n))] = send.astype(bf16)
    send_ref[(*at, slice(n, n + PAD))] = with_top(send, PAD).astype(bf16)


def weight_kernel(place_ref, tokens_ref, cotangent_ref, keep_ref, send_ref, total_ref):
    total_ref[...] = lax.dot_general(
        tokens_ref[...],
        cotangent_ref[...],
        (((0,), (0,)), ((), ())),
        preferred_element_type=f32,
    )
    for j in range(2):
        split_cores(place_ref[1], total_ref, j, 160, keep_ref, send_ref, (0, j))


def split_shapes(n):
    return [jax.ShapeDtypeStruct((2, 8, n + PAD, 384), kind) for kind in (f32, bf16)]


def weight_parts(yl, c, tokens, cotangent):
    block = pl.BlockSpec((1, 2, 160 + PAD, 384), lambda i, where: (where[0] ^ (i // 4), i % 4, 0, 0))
    return pl.pallas_call(
        weight_kernel,
        grid_spec=pltpu.PrefetchScalarGridSpec(
            num_scalar_prefetch=1,
            grid=(8,),
            in_specs=[
                pl.BlockSpec((512, 640), lambda i, where: (0, i)),
                pl.BlockSpec((512, 384), lambda i, where: (0, 0)),
            ],
            out_specs=[block, block],
            scratch_shapes=[pltpu.VMEM((640, 384), f32)],
        ),
        out_shape=split_shapes(160),
        compiler_params=pltpu.CompilerParams(vmem_limit_bytes=56 * MIB),
        cost_estimate=pl.CostEstimate(
            flops=2 * 512 * 5120 * 384, bytes_accessed=12 * MIB, transcendentals=0
        ),
    )(jnp.stack([yl, c]).astype(jnp.int32), tokens, cotangent)


def product(a, b, contract):
    return sum(
        lax.dot_general(u, v, (contract, ((), ())), preferred_element_type=f32)
        for u, v in ((a[0], b[0]), (a[0], b[1]), (a[1], b[0]))
    )


def share_kernel(place_ref, expanded_ref, grad_ref, keep_ref, send_ref, total_ref):
    grad = halves(grad_ref[...])
    for i in range(4):
        rows = slice(512 * i, 512 * i + 512)
        total_ref[rows] = product(halves(expanded_ref[:, rows]), grad, ((0,), (0,)))
    for j in range(16):
        split_cores(
            place_ref[1], total_ref, j, 64, keep_ref, send_ref, (place_ref[0] ^ (j // 8), j % 8)
        )


def share_parts(yl, c, expanded, grad):
    return pl.pallas_call(
        share_kernel,
        in_specs=[SMEM, VMEM, VMEM],
        out_specs=[VMEM, VMEM],
        out_shape=split_shapes(64),
        scratch_shapes=[pltpu.VMEM((2048, 384), f32)],
        compiler_params=pltpu.CompilerParams(vmem_limit_bytes=24 * MIB),
        cost_estimate=pl.CostEstimate(
            flops=6 * 160 * 2048 * 384, bytes_accessed=6 * MIB, transcendentals=0
        ),
    )(jnp.stack([yl, c]).astype(jnp.int32), expanded, grad)


def blocks_kernel(a_ref, b_ref, out_ref):
    a = halves(a_ref[...])
    n, m = a[0].shape[0], out_ref.shape[2]
    for q in range(8):
        b = b_ref[q * m : q * m + m, :]
        if b.dtype == bf16:
            total = sum(
                lax.dot_general(u, b, (((1,), (1,)), ((), ())), preferred_element_type=f32) for u in a
            )
        else:
            total = product(a, halves(b), ((1,), (1,)))
        out_ref[q, :n] = total
        out_ref[q, n:] = with_top(total, PAD)


def blocks_of(a, b):
    n, m = a.shape[0], b.shape[0] // 8
    return pl.pallas_call(
        blocks_kernel,
        in_specs=[VMEM, VMEM],
        out_specs=VMEM,
        out_shape=jax.ShapeDtypeStruct((8, n + PAD, m), f32),
        compiler_params=pltpu.CompilerParams(vmem_limit_bytes=24 * MIB),
        cost_estimate=pl.CostEstimate(
            flops=6 * a.shape[0] * b.size, bytes_accessed=6 * MIB, transcendentals=0
        ),
    )(a, b)


def shards(tokens, cotangent, teacher, expand_model, expand_heads):
    yl, z, c = [lax.axis_index(name) for name in ROW]
    yh, x = [lax.axis_index(name) for name in COL]

    packed = pair_y(pack_teacher_heads(teacher, expand_heads.T), yl)
    tokens_late = after(tokens, packed)
    sent, own = sum_mates(*weight_parts(yl, c, tokens_late, cotangent))
    packed = after(gather_z(packed), sent)
    model_two = after(pair_col(expand_model), sent)

    shapes = [jax.ShapeDtypeStruct((32, 128, 256), bf16), jax.ShapeDtypeStruct((32, 64, 384), f32)]
    teacher_block, heads = weave(packed, c, shapes, put_teacher_heads)
    teacher_block, heads = teacher_block.reshape(4096, 256), heads.reshape(2048, 384)
    model_rows = gather_col(model_two, yh, x)
    expanded_two = pair_col(jnp.dot(model_rows, teacher_block.astype(f32), precision=HIGH))
    expanded = gather_col(expanded_two, yh, x)
    blocks = lax.all_to_all(blocks_z(sent, own), "z", 0, 0, tiled=True)

    student = jnp.dot(expanded, heads, precision=HIGH).astype(bf16)
    student_two = pair_y(student, yl)
    student_own = gather_z(student_two)

    grad = jnp.sum(dec(after(blocks, student)), axis=0)
    sent, own = sum_mates(*share_parts(yl, c, expanded, grad))
    side = swap_col(payload(blocks_of(grad, heads)))
    side = jnp.sum(dec(after(side, sent, student_two)), axis=0)
    blocks = payload(blocks_of(side, teacher_block))
    grad_model = jnp.sum(dec(swap_col(blocks)), axis=0)
    shares = parts_z(after(blocks_z(sent, own), blocks), z)
    grad_heads = sum(dec(p) for p in shares).T

    shape = jax.ShapeDtypeStruct((32, 160, 384), bf16)
    student = weave(after(student_own, blocks), c, shape, put_rows, 4).reshape(5120, 384)
    queries = jnp.dot(tokens, student, preferred_element_type=f32)
    return (queries, grad_model, grad_heads)


def solution(mesh):
    mesh = Mesh(mesh.devices.reshape(2, 8, 2, 2, 4), ROW + COL)
    in_specs = (P(ROW, None), P(ROW, COL), P(ROW, COL), P(ROW, COL), P(COL, ROW))
    out_specs = (P(ROW, COL), P(ROW, COL), P(COL, ROW))
    return jax.shard_map(
        shards, mesh=mesh, in_specs=in_specs, out_specs=out_specs, check_vma=False
    )
```

```python
import jax
import jax.numpy as jnp
from jax import lax
from jax.experimental import pallas as pl
from jax.experimental.pallas import tpu as pltpu
from jax.sharding import Mesh, PartitionSpec as P

f32, f16, bf16 = jnp.float32, jnp.float16, jnp.bfloat16
HIGH = lax.Precision.HIGH
PAD = 16
TOP = 14.0
ROW, COL = ("yl", "z", "c"), ("yh", "x")
MIB = 2**20
VMEM, SMEM = pl.BlockSpec(memory_space=pltpu.VMEM), pl.BlockSpec(memory_space=pltpu.SMEM)


def swap(a, axis):
    return lax.ppermute(a, axis, [(0, 1), (1, 0)])


def after(a, *others):
    return lax.optimization_barrier((a, *others))[0]


def scale_of(top):
    return jnp.ceil(jnp.log2(jnp.maximum(top, 2.0**-100)))


def rows_of(a):
    return lax.broadcasted_iota(jnp.int32, a.shape, a.ndim - 2)


def payload(a):
    n = a.shape[-2] - PAD
    k = scale_of(a[..., n : n + 1, :])
    return jnp.where(rows_of(a) < n, a * jnp.exp2(TOP - k), k).astype(f16)


def dec(p):
    return p[..., :-PAD, :].astype(f32) * jnp.exp2(p[..., -1:, :].astype(f32) - TOP)


def enc(a):
    wide = jnp.pad(a, [(0, PAD), (0, 0)])
    k = scale_of(jnp.max(jnp.abs(a)))
    return jnp.where(rows_of(wide) < a.shape[0], wide * jnp.exp2(TOP - k), k).astype(f16)


def halves(a):
    high = a.astype(bf16)
    return high, (a - high.astype(f32)).astype(bf16)


def halves_outside(a):
    high = lax.reduce_precision(a, 8, 7)
    return high.astype(bf16), (a - high).astype(bf16)


def pair_y(a, yl):
    mate = swap(a, "yl")
    return jnp.stack([jnp.where(yl == 0, a, mate), jnp.where(yl == 0, mate, a)])


def gather_z(two):
    return lax.all_gather(two, "z").reshape((16,) + two.shape[1:])


def place(where, parts, shape, put):
    def kernel(where_ref, *refs):
        i = 0
        for src in refs[: len(parts)]:
            for j in range(src.shape[0]):
                put(refs[len(parts) :], where_ref[i], src[j])
                i += 1

    return pl.pallas_call(
        kernel,
        out_shape=shape,
        in_specs=[SMEM] + [VMEM] * len(parts),
        out_specs=jax.tree.map(lambda _: VMEM, shape),
        compiler_params=pltpu.CompilerParams(vmem_limit_bytes=24 * MIB),
    )(jnp.stack(where).astype(jnp.int32), *parts)


def put_rows(outs, at, block):
    outs[0][at] = block


def put_columns(outs, at, block):
    m = block.shape[1]
    outs[0][:, pl.ds(pl.multiple_of(at * m, 128), m)] = block


def put_heads(outs, at, block):
    both = block[:96].astype(f32) + block[96:].astype(f32)
    outs[0][at, :, :256] = both[:64]
    outs[0][at, :32, 256:] = both[64:, :128]
    outs[0][at, 32:, 256:] = both[64:, 128:]


def pack_teacher_heads(teacher, heads_t):
    rows = [teacher]
    for half in halves_outside(heads_t):
        rows += [half[:, :256], jnp.concatenate([half[:32, 256:], half[32:, 256:]], axis=1)]
    return jnp.concatenate(rows)


def weave(own, c, shape, put, pieces=1):
    where = [i * 16 + z * 2 + k for k in (c, 1 - c) for z in range(8) for i in (0, 1)]
    mine = jnp.split(own, pieces)
    return place(where, mine + [swap(p, "c") for p in mine], shape, put)


def pair_col(a):
    p = enc(a)
    return jnp.stack([p, swap(p, "yh")])


def gather_col(two, yh, x):
    parts = [two]
    parts += [lax.ppermute(two, "x", [(i, (i + d) % 4) for i in range(4)]) for d in (1, -1, 2)]
    where = [(yh ^ j) * 4 + ((x - d) & 3) for d in (0, 1, -1, 2) for j in (0, 1)]
    n, m = two.shape[1] - PAD, two.shape[2]
    shape = jax.ShapeDtypeStruct((n, 8 * m), f32)
    return place(where, [dec(p) for p in parts], shape, put_columns)


def swap_col(blocks):
    return lax.all_to_all(blocks, COL, 0, 0, tiled=True)


def sum_mates(keep, send):
    x = keep + swap(send, "c").astype(f32)
    return payload(x[1]), x[0]


def blocks_z(sent, own):
    mate = swap(sent, "yl")
    n = own.shape[1] - PAD
    k = mate[:, n : n + 1].astype(f32)
    got = jnp.where(rows_of(own) < n, mate.astype(f32) * jnp.exp2(k - TOP), jnp.exp2(k))
    return payload(own + got)


def parts_z(blocks, z):
    got = [lax.dynamic_index_in_dim(blocks, z, 0, keepdims=False)]
    for d in range(1, 8):
        block = lax.dynamic_index_in_dim(blocks, (z + d) & 7, 0, keepdims=False)
        got.append(lax.ppermute(block, "z", [(i, (i + d) % 8) for i in range(8)]))
    return got


def with_top(a, rows):
    return jnp.broadcast_to(jnp.max(jnp.abs(a), axis=0, keepdims=True), (rows, a.shape[1]))


def split_cores(core, total_ref, j, n, keep_ref, send_ref, at):
    keep = total_ref[pl.ds(pl.multiple_of(2 * n * j + n * core, 8), n), :]
    send = total_ref[pl.ds(pl.multiple_of(2 * n * j + n * (1 - core), 8), n), :]
    keep_ref[(*at, slice(0, n))] = keep
    keep_ref[(*at, slice(n, n + PAD))] = with_top(keep, PAD)
    send_ref[(*at, slice(0, n))] = send.astype(bf16)
    send_ref[(*at, slice(n, n + PAD))] = with_top(send, PAD).astype(bf16)


def weight_kernel(place_ref, tokens_ref, cotangent_ref, keep_ref, send_ref, total_ref):
    total_ref[...] = lax.dot_general(
        tokens_ref[...],
        cotangent_ref[...],
        (((0,), (0,)), ((), ())),
        preferred_element_type=f32,
    )
    for j in range(2):
        split_cores(place_ref[0], total_ref, j, 160, keep_ref, send_ref, (0, j))


def split_shapes(n):
    return [jax.ShapeDtypeStruct((2, 8, n + PAD, 384), kind) for kind in (f32, bf16)]


def weight_parts(c, tokens, cotangent):
    block = pl.BlockSpec((1, 2, 160 + PAD, 384), lambda i, where: (i // 4, i % 4, 0, 0))
    return pl.pallas_call(
        weight_kernel,
        grid_spec=pltpu.PrefetchScalarGridSpec(
            num_scalar_prefetch=1,
            grid=(8,),
            in_specs=[
                pl.BlockSpec((512, 640), lambda i, where: (0, i)),
                pl.BlockSpec((512, 384), lambda i, where: (0, 0)),
            ],
            out_specs=[block, block],
            scratch_shapes=[pltpu.VMEM((640, 384), f32)],
        ),
        out_shape=split_shapes(160),
        compiler_params=pltpu.CompilerParams(vmem_limit_bytes=56 * MIB),
        cost_estimate=pl.CostEstimate(
            flops=2 * 512 * 5120 * 384, bytes_accessed=12 * MIB, transcendentals=0
        ),
    )(c[None].astype(jnp.int32), tokens, cotangent)


def product(a, b, contract):
    return sum(
        lax.dot_general(u, v, (contract, ((), ())), preferred_element_type=f32)
        for u, v in ((a[0], b[0]), (a[0], b[1]), (a[1], b[0]))
    )


def share_kernel(place_ref, expanded_ref, grad_ref, keep_ref, send_ref, total_ref):
    grad = halves(grad_ref[...])
    for i in range(4):
        rows = slice(512 * i, 512 * i + 512)
        total_ref[rows] = product(halves(expanded_ref[:, rows]), grad, ((0,), (0,)))
    for j in range(16):
        split_cores(
            place_ref[1], total_ref, j, 64, keep_ref, send_ref, (place_ref[0] ^ (j // 8), j % 8)
        )


def share_parts(yl, c, expanded, grad):
    return pl.pallas_call(
        share_kernel,
        in_specs=[SMEM, VMEM, VMEM],
        out_specs=[VMEM, VMEM],
        out_shape=split_shapes(64),
        scratch_shapes=[pltpu.VMEM((2048, 384), f32)],
        compiler_params=pltpu.CompilerParams(vmem_limit_bytes=24 * MIB),
        cost_estimate=pl.CostEstimate(
            flops=6 * 160 * 2048 * 384, bytes_accessed=6 * MIB, transcendentals=0
        ),
    )(jnp.stack([yl, c]).astype(jnp.int32), expanded, grad)


def blocks_kernel(a_ref, b_ref, out_ref):
    a = halves(a_ref[...])
    n, m = a[0].shape[0], out_ref.shape[2]
    for q in range(8):
        b = b_ref[q * m : q * m + m, :]
        if b.dtype == bf16:
            total = sum(
                lax.dot_general(u, b, (((1,), (1,)), ((), ())), preferred_element_type=f32) for u in a
            )
        else:
            total = product(a, halves(b), ((1,), (1,)))
        out_ref[q, :n] = total
        out_ref[q, n:] = with_top(total, PAD)


def blocks_of(a, b):
    n, m = a.shape[0], b.shape[0] // 8
    return pl.pallas_call(
        blocks_kernel,
        in_specs=[VMEM, VMEM],
        out_specs=VMEM,
        out_shape=jax.ShapeDtypeStruct((8, n + PAD, m), f32),
        compiler_params=pltpu.CompilerParams(vmem_limit_bytes=24 * MIB),
        cost_estimate=pl.CostEstimate(
            flops=6 * a.shape[0] * b.size, bytes_accessed=6 * MIB, transcendentals=0
        ),
    )(a, b)


def shards(tokens, cotangent, teacher, expand_model, expand_heads):
    yl, z, c = [lax.axis_index(name) for name in ROW]
    yh, x = [lax.axis_index(name) for name in COL]

    packed = pair_y(pack_teacher_heads(teacher, expand_heads.T), yl)
    tokens_late = after(tokens, packed)
    keep, send = weight_parts(c, tokens_late, cotangent)
    blocks = payload(keep + swap(send, "c").astype(f32)).reshape(16, 160 + PAD, 384)
    packed = after(gather_z(packed), blocks)
    model_two = after(pair_col(expand_model), blocks)
    blocks = lax.all_to_all(blocks, ("yl", "z"), 0, 0, tiled=True)

    shape = jax.ShapeDtypeStruct((32, 128, 256), bf16)
    teacher_block = weave(packed[:, :128], c, shape, put_rows).reshape(4096, 256)
    shape = jax.ShapeDtypeStruct((32, 64, 384), f32)
    heads = weave(packed[:, 128:], c, shape, put_heads).reshape(2048, 384)
    model_rows = gather_col(model_two, yh, x)
    expanded_two = pair_col(jnp.dot(model_rows, teacher_block.astype(f32), precision=HIGH))
    expanded = gather_col(expanded_two, yh, x)

    student = jnp.dot(expanded, heads, precision=HIGH).astype(bf16)
    student_two = pair_y(student, yl)
    student_own = gather_z(student_two)

    grad = jnp.sum(dec(after(blocks, student)), axis=0)
    blocks = after(payload(blocks_of(grad, heads)), student_two)
    side = swap_col(blocks)
    sent, own = sum_mates(*share_parts(yl, c, after(expanded, blocks), grad))
    side = jnp.sum(dec(after(side, sent)), axis=0)
    blocks = payload(blocks_of(side, teacher_block))
    grad_model = jnp.sum(dec(swap_col(blocks)), axis=0)
    shares = parts_z(after(blocks_z(sent, own), blocks), z)
    grad_heads = sum(dec(p) for p in shares).T

    shape = jax.ShapeDtypeStruct((32, 160, 384), bf16)
    student = weave(after(student_own, blocks), c, shape, put_rows, 4).reshape(5120, 384)
    queries = jnp.dot(tokens, student, preferred_element_type=f32)
    return (queries, grad_model, grad_heads)


def solution(mesh):
    mesh = Mesh(mesh.devices.reshape(2, 8, 2, 2, 4), ROW + COL)
    in_specs = (P(ROW, None), P(ROW, COL), P(ROW, COL), P(ROW, COL), P(COL, ROW))
    out_specs = (P(ROW, COL), P(ROW, COL), P(COL, ROW))
    return jax.shard_map(
        shards, mesh=mesh, in_specs=in_specs, out_specs=out_specs, check_vma=False
    )
```

```python
import jax
import jax.numpy as jnp
from jax import lax
from jax.experimental import pallas as pl
from jax.experimental.pallas import tpu as pltpu
from jax.sharding import Mesh, PartitionSpec as P

f32, f16, bf16 = jnp.float32, jnp.float16, jnp.bfloat16
HIGH = lax.Precision.HIGH
PAD = 16
KEY = 8
TOP = 14.0
ROW, COL = ("yl", "z", "c"), ("yh", "x")
MIB = 2**20
VMEM, SMEM = pl.BlockSpec(memory_space=pltpu.VMEM), pl.BlockSpec(memory_space=pltpu.SMEM)


def swap(a, axis):
    return lax.ppermute(a, axis, [(0, 1), (1, 0)])


def after(a, *others):
    return lax.optimization_barrier((a, *others))[0]


def scale_of(top):
    return jnp.ceil(jnp.log2(jnp.maximum(top, 2.0**-100)))


def rows_of(a):
    return lax.broadcasted_iota(jnp.int32, a.shape, a.ndim - 2)


def payload(a):
    n = a.shape[-2] - a.shape[-2] % 32
    a = a[..., : n + KEY, :]
    k = scale_of(a[..., n : n + 1, :])
    return jnp.where(rows_of(a) < n, a * jnp.exp2(TOP - k), k).astype(f16)


def dec(p):
    return p[..., :-KEY, :].astype(f32) * jnp.exp2(p[..., -1:, :].astype(f32) - TOP)


def enc(a):
    wide = jnp.pad(a, [(0, KEY), (0, 0)])
    k = scale_of(jnp.max(jnp.abs(a)))
    return jnp.where(rows_of(wide) < a.shape[0], wide * jnp.exp2(TOP - k), k).astype(f16)


def halves(a):
    high = a.astype(bf16)
    return high, (a - high.astype(f32)).astype(bf16)


def halves_outside(a):
    high = lax.reduce_precision(a, 8, 7)
    return high.astype(bf16), (a - high).astype(bf16)


def pair_y(a, yl):
    mate = swap(a, "yl")
    return jnp.stack([jnp.where(yl == 0, a, mate), jnp.where(yl == 0, mate, a)])


def gather_z(two):
    return lax.all_gather(two, "z").reshape((16,) + two.shape[1:])


def place(where, parts, shape, put):
    def kernel(where_ref, *refs):
        i = 0
        for src in refs[: len(parts)]:
            for j in range(src.shape[0]):
                put(refs[len(parts) :], where_ref[i], src[j])
                i += 1

    return pl.pallas_call(
        kernel,
        out_shape=shape,
        in_specs=[SMEM] + [VMEM] * len(parts),
        out_specs=jax.tree.map(lambda _: VMEM, shape),
        compiler_params=pltpu.CompilerParams(vmem_limit_bytes=24 * MIB),
    )(jnp.stack(where).astype(jnp.int32), *parts)


def put_rows(outs, at, block):
    outs[0][at] = block


def put_columns(outs, at, block):
    m = block.shape[1]
    outs[0][:, pl.ds(pl.multiple_of(at * m, 128), m)] = block


def put_teacher_heads(outs, at, block):
    teacher, heads = outs
    teacher[at] = block[:128]
    both = block[128:224].astype(f32) + block[224:].astype(f32)
    heads[at, :, :256] = both[:64]
    heads[at, :32, 256:] = both[64:, :128]
    heads[at, 32:, 256:] = both[64:, 128:]


def pack_teacher_heads(teacher, heads_t):
    rows = [teacher]
    for half in halves_outside(heads_t):
        rows += [half[:, :256], jnp.concatenate([half[:32, 256:], half[32:, 256:]], axis=1)]
    return jnp.concatenate(rows)


def weave(own, c, shape, put, pieces=1):
    where = [i * 16 + z * 2 + k for k in (c, 1 - c) for z in range(8) for i in (0, 1)]
    mine = jnp.split(own, pieces)
    return place(where, mine + [swap(p, "c") for p in mine], shape, put)


def pair_col(a):
    p = enc(a)
    return jnp.stack([p, swap(p, "yh")])


def gather_col(two, yh, x):
    parts = [two]
    parts += [lax.ppermute(two, "x", [(i, (i + d) % 4) for i in range(4)]) for d in (1, -1, 2)]
    where = [(yh ^ j) * 4 + ((x - d) & 3) for d in (0, 1, -1, 2) for j in (0, 1)]
    n, m = two.shape[1] - KEY, two.shape[2]
    shape = jax.ShapeDtypeStruct((n, 8 * m), f32)
    return place(where, [dec(p) for p in parts], shape, put_columns)


def swap_col(blocks):
    return lax.all_to_all(blocks, COL, 0, 0, tiled=True)


def sum_mates(keep, send):
    got = swap(send, "c")
    return payload(keep[1] + got[1].astype(f32)), (keep[0], got[0])


def blocks_z(sent, own):
    mate = swap(sent, "yl")
    n = mate.shape[1] - KEY
    k = mate[:, n : n + 1].astype(f32)
    got = jnp.where(rows_of(mate) < n, mate.astype(f32) * jnp.exp2(k - TOP), jnp.exp2(k))
    return payload(own[0][:, : n + KEY] + own[1][:, : n + KEY].astype(f32) + got)


def parts_z(blocks, z):
    got = [lax.dynamic_index_in_dim(blocks, z, 0, keepdims=False)]
    for d in range(1, 8):
        block = lax.dynamic_index_in_dim(blocks, (z + d) & 7, 0, keepdims=False)
        got.append(lax.ppermute(block, "z", [(i, (i + d) % 8) for i in range(8)]))
    return got


def with_top(a, rows):
    return jnp.broadcast_to(jnp.max(jnp.abs(a), axis=0, keepdims=True), (rows, a.shape[1]))


def split_cores(core, total_ref, j, n, keep_ref, send_ref, at):
    keep = total_ref[pl.ds(pl.multiple_of(2 * n * j + n * core, 8), n), :]
    send = total_ref[pl.ds(pl.multiple_of(2 * n * j + n * (1 - core), 8), n), :]
    keep_ref[(*at, slice(0, n))] = keep
    keep_ref[(*at, slice(n, n + PAD))] = with_top(keep, PAD)
    send_ref[(*at, slice(0, n))] = send.astype(bf16)
    send_ref[(*at, slice(n, n + PAD))] = with_top(send, PAD).astype(bf16)


def weight_kernel(place_ref, tokens_ref, cotangent_ref, keep_ref, send_ref, total_ref):
    total_ref[...] = lax.dot_general(
        tokens_ref[...],
        cotangent_ref[...],
        (((0,), (0,)), ((), ())),
        preferred_element_type=f32,
    )
    for j in range(2):
        split_cores(place_ref[1], total_ref, j, 160, keep_ref, send_ref, (0, j))


def split_shapes(n):
    return [jax.ShapeDtypeStruct((2, 8, n + PAD, 384), kind) for kind in (f32, bf16)]


def weight_parts(yl, c, tokens, cotangent):
    block = pl.BlockSpec((1, 2, 160 + PAD, 384), lambda i, where: (where[0] ^ (i // 4), i % 4, 0, 0))
    return pl.pallas_call(
        weight_kernel,
        grid_spec=pltpu.PrefetchScalarGridSpec(
            num_scalar_prefetch=1,
            grid=(8,),
            in_specs=[
                pl.BlockSpec((512, 640), lambda i, where: (0, i)),
                pl.BlockSpec((512, 384), lambda i, where: (0, 0)),
            ],
            out_specs=[block, block],
            scratch_shapes=[pltpu.VMEM((640, 384), f32)],
        ),
        out_shape=split_shapes(160),
        compiler_params=pltpu.CompilerParams(vmem_limit_bytes=56 * MIB),
        cost_estimate=pl.CostEstimate(
            flops=2 * 512 * 5120 * 384, bytes_accessed=12 * MIB, transcendentals=0
        ),
    )(jnp.stack([yl, c]).astype(jnp.int32), tokens, cotangent)


def product(a, b, contract):
    return sum(
        lax.dot_general(u, v, (contract, ((), ())), preferred_element_type=f32)
        for u, v in ((a[0], b[0]), (a[0], b[1]), (a[1], b[0]))
    )


def share_kernel(place_ref, expanded_ref, grad_ref, keep_ref, send_ref, total_ref):
    grad = halves(grad_ref[...])
    for i in range(4):
        rows = slice(512 * i, 512 * i + 512)
        total_ref[rows] = product(halves(expanded_ref[:, rows]), grad, ((0,), (0,)))
    for j in range(16):
        split_cores(
            place_ref[1], total_ref, j, 64, keep_ref, send_ref, (place_ref[0] ^ (j // 8), j % 8)
        )


def share_parts(yl, c, expanded, grad):
    return pl.pallas_call(
        share_kernel,
        in_specs=[SMEM, VMEM, VMEM],
        out_specs=[VMEM, VMEM],
        out_shape=split_shapes(64),
        scratch_shapes=[pltpu.VMEM((2048, 384), f32)],
        compiler_params=pltpu.CompilerParams(vmem_limit_bytes=24 * MIB),
        cost_estimate=pl.CostEstimate(
            flops=6 * 160 * 2048 * 384, bytes_accessed=6 * MIB, transcendentals=0
        ),
    )(jnp.stack([yl, c]).astype(jnp.int32), expanded, grad)


def blocks_kernel(a_ref, b_ref, out_ref):
    a = halves(a_ref[...])
    n, m = a[0].shape[0], out_ref.shape[2]
    for q in range(8):
        b = b_ref[q * m : q * m + m, :]
        if b.dtype == bf16:
            total = sum(
                lax.dot_general(u, b, (((1,), (1,)), ((), ())), preferred_element_type=f32) for u in a
            )
        else:
            total = product(a, halves(b), ((1,), (1,)))
        out_ref[q, :n] = total
        out_ref[q, n:] = with_top(total, PAD)


def blocks_of(a, b):
    n, m = a.shape[0], b.shape[0] // 8
    return pl.pallas_call(
        blocks_kernel,
        in_specs=[VMEM, VMEM],
        out_specs=VMEM,
        out_shape=jax.ShapeDtypeStruct((8, n + PAD, m), f32),
        compiler_params=pltpu.CompilerParams(vmem_limit_bytes=24 * MIB),
        cost_estimate=pl.CostEstimate(
            flops=6 * a.shape[0] * b.size, bytes_accessed=6 * MIB, transcendentals=0
        ),
    )(a, b)


def shards(tokens, cotangent, teacher, expand_model, expand_heads):
    yl, z, c = [lax.axis_index(name) for name in ROW]
    yh, x = [lax.axis_index(name) for name in COL]

    packed = pair_y(pack_teacher_heads(teacher, expand_heads.T), yl)
    tokens_late = after(tokens, packed)
    sent, own = sum_mates(*weight_parts(yl, c, tokens_late, cotangent))
    packed = after(gather_z(packed), sent)
    model_two = after(pair_col(expand_model), sent)

    shapes = [jax.ShapeDtypeStruct((32, 128, 256), bf16), jax.ShapeDtypeStruct((32, 64, 384), f32)]
    teacher_block, heads = weave(packed, c, shapes, put_teacher_heads)
    teacher_block, heads = teacher_block.reshape(4096, 256), heads.reshape(2048, 384)
    model_rows = gather_col(model_two, yh, x)
    expanded_two = pair_col(jnp.dot(model_rows, teacher_block.astype(f32), precision=HIGH))
    expanded = gather_col(expanded_two, yh, x)
    blocks = lax.all_to_all(blocks_z(sent, own), "z", 0, 0, tiled=True)

    student = jnp.dot(expanded, heads, precision=HIGH).astype(bf16)
    student_two = pair_y(student, yl)
    student_own = gather_z(student_two)

    grad = jnp.sum(dec(after(blocks, student)), axis=0)
    sent, own = sum_mates(*share_parts(yl, c, expanded, grad))
    side = swap_col(payload(blocks_of(grad, heads)))
    side = jnp.sum(dec(after(side, sent, student_two)), axis=0)
    blocks = payload(blocks_of(side, teacher_block))
    grad_model = jnp.sum(dec(swap_col(blocks)), axis=0)
    shares = parts_z(after(blocks_z(sent, own), blocks), z)
    grad_heads = sum(dec(p) for p in shares).T

    shape = jax.ShapeDtypeStruct((32, 160, 384), bf16)
    student = weave(after(student_own, blocks), c, shape, put_rows, 4).reshape(5120, 384)
    queries = jnp.dot(tokens, student, preferred_element_type=f32)
    return (queries, grad_model, grad_heads)


def solution(mesh):
    mesh = Mesh(mesh.devices.reshape(2, 8, 2, 2, 4), ROW + COL)
    in_specs = (P(ROW, None), P(ROW, COL), P(ROW, COL), P(ROW, COL), P(COL, ROW))
    out_specs = (P(ROW, COL), P(ROW, COL), P(COL, ROW))
    return jax.shard_map(
        shards, mesh=mesh, in_specs=in_specs, out_specs=out_specs, check_vma=False
    )
```

```python
import jax
import jax.numpy as jnp
from jax import lax
from jax.experimental import pallas as pl
from jax.experimental.pallas import tpu as pltpu
from jax.sharding import Mesh, PartitionSpec as P

f32, f16, bf16 = jnp.float32, jnp.float16, jnp.bfloat16
HIGH = lax.Precision.HIGH
PAD = 16
KEY = 8
TOP = 14.0
ROW, COL = ("yl", "z", "c"), ("yh", "x")
MIB = 2**20
VMEM, SMEM = pl.BlockSpec(memory_space=pltpu.VMEM), pl.BlockSpec(memory_space=pltpu.SMEM)


def swap(a, axis):
    return lax.ppermute(a, axis, [(0, 1), (1, 0)])


def after(a, *others):
    return lax.optimization_barrier((a, *others))[0]


def scale_of(top):
    return jnp.ceil(jnp.log2(jnp.maximum(top, 2.0**-100)))


def rows_of(a):
    return lax.broadcasted_iota(jnp.int32, a.shape, a.ndim - 2)


def payload(a):
    n = a.shape[-2] - a.shape[-2] % 32
    a = a[..., : n + KEY, :]
    k = scale_of(a[..., n : n + 1, :])
    return jnp.where(rows_of(a) < n, a * jnp.exp2(TOP - k), k).astype(f16)


def dec(p):
    return p[..., :-KEY, :].astype(f32) * jnp.exp2(p[..., -1:, :].astype(f32) - TOP)


def enc(a):
    wide = jnp.pad(a, [(0, KEY), (0, 0)])
    k = scale_of(jnp.max(jnp.abs(a)))
    return jnp.where(rows_of(wide) < a.shape[0], wide * jnp.exp2(TOP - k), k).astype(f16)


def halves(a):
    high = a.astype(bf16)
    return high, (a - high.astype(f32)).astype(bf16)


def halves_outside(a):
    high = lax.reduce_precision(a, 8, 7)
    return high.astype(bf16), (a - high).astype(bf16)


def pair_y(a, yl):
    mate = swap(a, "yl")
    return jnp.stack([jnp.where(yl == 0, a, mate), jnp.where(yl == 0, mate, a)])


def gather_z(two):
    return lax.all_gather(two, "z").reshape((16,) + two.shape[1:])


def place(where, parts, shape, put):
    def kernel(where_ref, *refs):
        i = 0
        for src in refs[: len(parts)]:
            for j in range(src.shape[0]):
                put(refs[len(parts) :], where_ref[i], src[j])
                i += 1

    return pl.pallas_call(
        kernel,
        out_shape=shape,
        in_specs=[SMEM] + [VMEM] * len(parts),
        out_specs=jax.tree.map(lambda _: VMEM, shape),
        compiler_params=pltpu.CompilerParams(vmem_limit_bytes=24 * MIB),
    )(jnp.stack(where).astype(jnp.int32), *parts)


def put_rows(outs, at, block):
    outs[0][at] = block


def put_columns(outs, at, block):
    m = block.shape[1]
    outs[0][:, pl.ds(pl.multiple_of(at * m, 128), m)] = block


def put_teacher_heads(outs, at, block):
    teacher, heads = outs
    teacher[at] = block[:128]
    both = block[128:224].astype(f32) + block[224:].astype(f32)
    heads[at, :, :256] = both[:64]
    heads[at, :32, 256:] = both[64:, :128]
    heads[at, 32:, 256:] = both[64:, 128:]


def pack_teacher_heads(teacher, heads_t):
    rows = [teacher]
    for half in halves_outside(heads_t):
        rows += [half[:, :256], jnp.concatenate([half[:32, 256:], half[32:, 256:]], axis=1)]
    return jnp.concatenate(rows)


def weave(own, c, shape, put, pieces=1):
    where = [i * 16 + z * 2 + k for k in (c, 1 - c) for z in range(8) for i in (0, 1)]
    mine = jnp.split(own, pieces)
    return place(where, mine + [swap(p, "c") for p in mine], shape, put)


def pair_col(a):
    p = enc(a)
    return jnp.stack([p, swap(p, "yh")])


def gather_col(two, yh, x):
    parts = [two]
    parts += [lax.ppermute(two, "x", [(i, (i + d) % 4) for i in range(4)]) for d in (1, -1, 2)]
    where = [(yh ^ j) * 4 + ((x - d) & 3) for d in (0, 1, -1, 2) for j in (0, 1)]
    n, m = two.shape[1] - KEY, two.shape[2]
    shape = jax.ShapeDtypeStruct((n, 8 * m), f32)
    return place(where, [dec(p) for p in parts], shape, put_columns)


def swap_col(blocks):
    return lax.all_to_all(blocks, COL, 0, 0, tiled=True)


def sum_mates(keep, keep_mate, send):
    got = swap(send, "c")
    return payload(keep_mate + got[1].astype(f32)), (keep, got[0])


def blocks_z(sent, own):
    mate = swap(sent, "yl")
    n = mate.shape[1] - KEY
    k = mate[:, n : n + 1].astype(f32)
    got = jnp.where(rows_of(mate) < n, mate.astype(f32) * jnp.exp2(k - TOP), jnp.exp2(k))
    return payload(own[0][:, : n + KEY] + own[1][:, : n + KEY].astype(f32) + got)


def parts_z(blocks, z):
    got = [lax.dynamic_index_in_dim(blocks, z, 0, keepdims=False)]
    for d in range(1, 8):
        block = lax.dynamic_index_in_dim(blocks, (z + d) & 7, 0, keepdims=False)
        got.append(lax.ppermute(block, "z", [(i, (i + d) % 8) for i in range(8)]))
    return got


def with_top(a, rows):
    return jnp.broadcast_to(jnp.max(jnp.abs(a), axis=0, keepdims=True), (rows, a.shape[1]))


def split_cores(core, total_ref, j, n, keep_ref, send_ref, keep_at, send_at):
    keep = total_ref[pl.ds(pl.multiple_of(2 * n * j + n * core, 8), n), :]
    send = total_ref[pl.ds(pl.multiple_of(2 * n * j + n * (1 - core), 8), n), :]
    keep_ref[keep_at, :n] = keep
    keep_ref[keep_at, n:] = with_top(keep, PAD)
    send_ref[(*send_at, slice(0, n))] = send.astype(bf16)
    send_ref[(*send_at, slice(n, n + PAD))] = with_top(send, PAD).astype(bf16)


def weight_kernel(place_ref, tokens_ref, cotangent_ref, keep_ref, mate_ref, send_ref, total_ref):
    total_ref[...] = lax.dot_general(
        tokens_ref[...],
        cotangent_ref[...],
        (((0,), (0,)), ((), ())),
        preferred_element_type=f32,
    )

    def write(to_ref):
        for j in range(2):
            split_cores(place_ref[1], total_ref, j, 160, to_ref, send_ref, j, (0, j))

    step = pl.program_id(0)
    pl.when(step < 4)(lambda: write(keep_ref))
    pl.when(step >= 4)(lambda: write(mate_ref))


def split_shapes(n):
    keep = jax.ShapeDtypeStruct((8, n + PAD, 384), f32)
    return [keep, keep, jax.ShapeDtypeStruct((2, 8, n + PAD, 384), bf16)]


def weight_parts(yl, c, tokens, cotangent):
    rows = 160 + PAD
    return pl.pallas_call(
        weight_kernel,
        grid_spec=pltpu.PrefetchScalarGridSpec(
            num_scalar_prefetch=1,
            grid=(8,),
            in_specs=[
                pl.BlockSpec((512, 640), lambda i, where: (0, (where[0] ^ (i // 4)) * 4 + i % 4)),
                pl.BlockSpec((512, 384), lambda i, where: (0, 0)),
            ],
            out_specs=[
                pl.BlockSpec((2, rows, 384), lambda i, where: (jnp.minimum(i, 3), 0, 0)),
                pl.BlockSpec((2, rows, 384), lambda i, where: (jnp.maximum(i - 4, 0), 0, 0)),
                pl.BlockSpec((1, 2, rows, 384), lambda i, where: (i // 4, i % 4, 0, 0)),
            ],
            scratch_shapes=[pltpu.VMEM((640, 384), f32)],
        ),
        out_shape=split_shapes(160),
        compiler_params=pltpu.CompilerParams(vmem_limit_bytes=56 * MIB),
        cost_estimate=pl.CostEstimate(
            flops=2 * 512 * 5120 * 384, bytes_accessed=12 * MIB, transcendentals=0
        ),
    )(jnp.stack([yl, c]).astype(jnp.int32), tokens, cotangent)


def product(a, b, contract):
    return sum(
        lax.dot_general(u, v, (contract, ((), ())), preferred_element_type=f32)
        for u, v in ((a[0], b[0]), (a[0], b[1]), (a[1], b[0]))
    )


def share_kernel(place_ref, expanded_ref, grad_ref, keep_ref, mate_ref, send_ref, total_ref):
    grad = halves(grad_ref[...])
    for i in range(4):
        rows = slice(512 * i, 512 * i + 512)
        total_ref[rows] = product(halves(expanded_ref[:, rows]), grad, ((0,), (0,)))
    for i, to_ref in enumerate((keep_ref, mate_ref)):
        for z in range(8):
            j = (place_ref[0] ^ i) * 8 + z
            split_cores(place_ref[1], total_ref, j, 64, to_ref, send_ref, z, (i, z))


def share_parts(yl, c, expanded, grad):
    return pl.pallas_call(
        share_kernel,
        in_specs=[SMEM, VMEM, VMEM],
        out_specs=[VMEM] * 3,
        out_shape=split_shapes(64),
        scratch_shapes=[pltpu.VMEM((2048, 384), f32)],
        compiler_params=pltpu.CompilerParams(vmem_limit_bytes=24 * MIB),
        cost_estimate=pl.CostEstimate(
            flops=6 * 160 * 2048 * 384, bytes_accessed=6 * MIB, transcendentals=0
        ),
    )(jnp.stack([yl, c]).astype(jnp.int32), expanded, grad)


def blocks_kernel(a_ref, b_ref, out_ref):
    a = halves(a_ref[...])
    n, m = a[0].shape[0], out_ref.shape[2]
    for q in range(8):
        b = b_ref[q * m : q * m + m, :]
        if b.dtype == bf16:
            total = sum(
                lax.dot_general(u, b, (((1,), (1,)), ((), ())), preferred_element_type=f32) for u in a
            )
        else:
            total = product(a, halves(b), ((1,), (1,)))
        out_ref[q, :n] = total
        out_ref[q, n:] = with_top(total, PAD)


def blocks_of(a, b):
    n, m = a.shape[0], b.shape[0] // 8
    return pl.pallas_call(
        blocks_kernel,
        in_specs=[VMEM, VMEM],
        out_specs=VMEM,
        out_shape=jax.ShapeDtypeStruct((8, n + PAD, m), f32),
        compiler_params=pltpu.CompilerParams(vmem_limit_bytes=24 * MIB),
        cost_estimate=pl.CostEstimate(
            flops=6 * a.shape[0] * b.size, bytes_accessed=6 * MIB, transcendentals=0
        ),
    )(a, b)


def shards(tokens, cotangent, teacher, expand_model, expand_heads):
    yl, z, c = [lax.axis_index(name) for name in ROW]
    yh, x = [lax.axis_index(name) for name in COL]

    packed = pair_y(pack_teacher_heads(teacher, expand_heads.T), yl)
    tokens_late = after(tokens, packed)
    sent, own = sum_mates(*weight_parts(yl, c, tokens_late, cotangent))
    packed = after(gather_z(packed), sent)
    model_two = after(pair_col(expand_model), sent)

    shapes = [jax.ShapeDtypeStruct((32, 128, 256), bf16), jax.ShapeDtypeStruct((32, 64, 384), f32)]
    teacher_block, heads = weave(packed, c, shapes, put_teacher_heads)
    teacher_block, heads = teacher_block.reshape(4096, 256), heads.reshape(2048, 384)
    model_rows = gather_col(model_two, yh, x)
    expanded_two = pair_col(jnp.dot(model_rows, teacher_block.astype(f32), precision=HIGH))
    expanded = gather_col(expanded_two, yh, x)
    blocks = lax.all_to_all(blocks_z(sent, own), "z", 0, 0, tiled=True)

    student = jnp.dot(expanded, heads, precision=HIGH).astype(bf16)
    student_two = pair_y(student, yl)
    student_own = gather_z(student_two)

    grad = jnp.sum(dec(after(blocks, student)), axis=0)
    sent, own = sum_mates(*share_parts(yl, c, expanded, grad))
    side = swap_col(payload(blocks_of(grad, heads)))
    side = jnp.sum(dec(after(side, sent, student_two)), axis=0)
    blocks = payload(blocks_of(side, teacher_block))
    grad_model = jnp.sum(dec(swap_col(blocks)), axis=0)
    shares = parts_z(after(blocks_z(sent, own), blocks), z)
    grad_heads = sum(dec(p) for p in shares).T

    shape = jax.ShapeDtypeStruct((32, 160, 384), bf16)
    student = weave(after(student_own, blocks), c, shape, put_rows, 4).reshape(5120, 384)
    queries = jnp.dot(tokens, student, preferred_element_type=f32)
    return (queries, grad_model, grad_heads)


def solution(mesh):
    mesh = Mesh(mesh.devices.reshape(2, 8, 2, 2, 4), ROW + COL)
    in_specs = (P(ROW, None), P(ROW, COL), P(ROW, COL), P(ROW, COL), P(COL, ROW))
    out_specs = (P(ROW, COL), P(ROW, COL), P(COL, ROW))
    return jax.shard_map(
        shards, mesh=mesh, in_specs=in_specs, out_specs=out_specs, check_vma=False
    )
```

```python
import jax
import jax.numpy as jnp
from jax import lax
from jax.experimental import pallas as pl
from jax.experimental.pallas import tpu as pltpu
from jax.sharding import Mesh, PartitionSpec as P

f32, f16, bf16 = jnp.float32, jnp.float16, jnp.bfloat16
HIGH = lax.Precision.HIGH
PAD = 16
KEY = 8
TOP = 14.0
ROW, COL = ("yl", "z", "c"), ("yh", "x")
MIB = 2**20
VMEM, SMEM = pl.BlockSpec(memory_space=pltpu.VMEM), pl.BlockSpec(memory_space=pltpu.SMEM)


def swap(a, axis):
    return lax.ppermute(a, axis, [(0, 1), (1, 0)])


def after(a, *others):
    return lax.optimization_barrier((a, *others))[0]


def scale_of(top):
    return jnp.ceil(jnp.log2(jnp.maximum(top, 2.0**-100)))


def rows_of(a):
    return lax.broadcasted_iota(jnp.int32, a.shape, a.ndim - 2)


def payload(a):
    n = a.shape[-2] - a.shape[-2] % 32
    a = a[..., : n + KEY, :]
    k = scale_of(a[..., n : n + 1, :])
    return jnp.where(rows_of(a) < n, a * jnp.exp2(TOP - k), k).astype(f16)


def dec(p):
    return p[..., :-KEY, :].astype(f32) * jnp.exp2(p[..., -1:, :].astype(f32) - TOP)


def enc(a):
    wide = jnp.pad(a, [(0, KEY), (0, 0)])
    k = scale_of(jnp.max(jnp.abs(a)))
    return jnp.where(rows_of(wide) < a.shape[0], wide * jnp.exp2(TOP - k), k).astype(f16)


def halves(a):
    high = a.astype(bf16)
    return high, (a - high.astype(f32)).astype(bf16)


def halves_outside(a):
    high = lax.reduce_precision(a, 8, 7)
    return high.astype(bf16), (a - high).astype(bf16)


def pair_y(a, yl):
    mate = swap(a, "yl")
    return jnp.stack([jnp.where(yl == 0, a, mate), jnp.where(yl == 0, mate, a)])


def gather_z(two):
    return lax.all_gather(two, "z").reshape((16,) + two.shape[1:])


def place(where, parts, shape, put):
    def kernel(where_ref, *refs):
        i = 0
        for src in refs[: len(parts)]:
            for j in range(src.shape[0]):
                put(refs[len(parts) :], where_ref[i], src[j])
                i += 1

    return pl.pallas_call(
        kernel,
        out_shape=shape,
        in_specs=[SMEM] + [VMEM] * len(parts),
        out_specs=jax.tree.map(lambda _: VMEM, shape),
        compiler_params=pltpu.CompilerParams(vmem_limit_bytes=24 * MIB),
    )(jnp.stack(where).astype(jnp.int32), *parts)


def put_rows(outs, at, block):
    outs[0][at] = block


def put_columns(outs, at, block):
    m = block.shape[1]
    outs[0][:, pl.ds(pl.multiple_of(at * m, 128), m)] = block


def put_teacher_heads(outs, at, block):
    teacher, heads = outs
    teacher[at] = block[:128]
    both = block[128:224].astype(f32) + block[224:].astype(f32)
    heads[at, :, :256] = both[:64]
    heads[at, :32, 256:] = both[64:, :128]
    heads[at, 32:, 256:] = both[64:, 128:]


def pack_teacher_heads(teacher, heads_t):
    rows = [teacher]
    for half in halves_outside(heads_t):
        rows += [half[:, :256], jnp.concatenate([half[:32, 256:], half[32:, 256:]], axis=1)]
    return jnp.concatenate(rows)


def weave(own, c, shape, put, pieces=1):
    where = [i * 16 + z * 2 + k for k in (c, 1 - c) for z in range(8) for i in (0, 1)]
    mine = jnp.split(own, pieces)
    return place(where, mine + [swap(p, "c") for p in mine], shape, put)


def pair_col(a):
    p = enc(a)
    return jnp.stack([p, swap(p, "yh")])


def gather_col(two, yh, x):
    parts = [two]
    parts += [lax.ppermute(two, "x", [(i, (i + d) % 4) for i in range(4)]) for d in (1, -1, 2)]
    where = [(yh ^ j) * 4 + ((x - d) & 3) for d in (0, 1, -1, 2) for j in (0, 1)]
    n, m = two.shape[1] - KEY, two.shape[2]
    shape = jax.ShapeDtypeStruct((n, 8 * m), f32)
    return place(where, [dec(p) for p in parts], shape, put_columns)


def swap_col(blocks):
    return lax.all_to_all(blocks, COL, 0, 0, tiled=True)


def sum_mates(keep, keep_mate, send):
    got = swap(send, "c")
    return payload(keep_mate + got[1].astype(f32)), (keep, got[0])


def blocks_z(sent, own):
    mate = swap(sent, "yl")
    n = mate.shape[1] - KEY
    k = mate[:, n : n + 1].astype(f32)
    got = jnp.where(rows_of(mate) < n, mate.astype(f32) * jnp.exp2(k - TOP), jnp.exp2(k))
    return payload(own[0][:, : n + KEY] + own[1][:, : n + KEY].astype(f32) + got)


def parts_z(blocks, z):
    got = [lax.dynamic_index_in_dim(blocks, z, 0, keepdims=False)]
    for d in range(1, 8):
        block = lax.dynamic_index_in_dim(blocks, (z + d) & 7, 0, keepdims=False)
        got.append(lax.ppermute(block, "z", [(i, (i + d) % 8) for i in range(8)]))
    return got


def with_top(a, rows):
    return jnp.broadcast_to(jnp.max(jnp.abs(a), axis=0, keepdims=True), (rows, a.shape[1]))


def split_cores(core, total_ref, j, n, keep_ref, send_ref, keep_at, send_at):
    keep = total_ref[pl.ds(pl.multiple_of(2 * n * j + n * core, 8), n), :]
    send = total_ref[pl.ds(pl.multiple_of(2 * n * j + n * (1 - core), 8), n), :]
    keep_ref[keep_at, :n] = keep
    keep_ref[keep_at, n:] = with_top(keep, PAD)
    send_ref[(*send_at, slice(0, n))] = send.astype(bf16)
    send_ref[(*send_at, slice(n, n + PAD))] = with_top(send, PAD).astype(bf16)


def weight_kernel(place_ref, tokens_ref, cotangent_ref, keep_ref, mate_ref, send_ref, total_ref):
    total_ref[...] = lax.dot_general(
        tokens_ref[...],
        cotangent_ref[...],
        (((0,), (0,)), ((), ())),
        preferred_element_type=f32,
    )

    def write(to_ref):
        for j in range(2):
            split_cores(place_ref[1], total_ref, j, 160, to_ref, send_ref, j, (0, j))

    step = pl.program_id(0)
    pl.when(step < 4)(lambda: write(keep_ref))
    pl.when(step >= 4)(lambda: write(mate_ref))


def split_shapes(n):
    keep = jax.ShapeDtypeStruct((8, n + PAD, 384), f32)
    return [keep, keep, jax.ShapeDtypeStruct((2, 8, n + PAD, 384), bf16)]


def weight_parts(yl, c, tokens, cotangent):
    rows = 160 + PAD
    return pl.pallas_call(
        weight_kernel,
        grid_spec=pltpu.PrefetchScalarGridSpec(
            num_scalar_prefetch=1,
            grid=(8,),
            in_specs=[
                pl.BlockSpec((512, 640), lambda i, where: (0, (where[0] ^ (i // 4)) * 4 + i % 4)),
                pl.BlockSpec((512, 384), lambda i, where: (0, 0)),
            ],
            out_specs=[
                pl.BlockSpec((2, rows, 384), lambda i, where: (jnp.minimum(i, 3), 0, 0)),
                pl.BlockSpec((2, rows, 384), lambda i, where: (jnp.maximum(i - 4, 0), 0, 0)),
                pl.BlockSpec((1, 2, rows, 384), lambda i, where: (i // 4, i % 4, 0, 0)),
            ],
            scratch_shapes=[pltpu.VMEM((640, 384), f32)],
        ),
        out_shape=split_shapes(160),
        compiler_params=pltpu.CompilerParams(vmem_limit_bytes=56 * MIB),
        cost_estimate=pl.CostEstimate(
            flops=2 * 512 * 5120 * 384, bytes_accessed=12 * MIB, transcendentals=0
        ),
    )(jnp.stack([yl, c]).astype(jnp.int32), tokens, cotangent)


def product(a, b, contract):
    return sum(
        lax.dot_general(u, v, (contract, ((), ())), preferred_element_type=f32)
        for u, v in ((a[0], b[0]), (a[0], b[1]), (a[1], b[0]))
    )


def share_kernel(place_ref, expanded_ref, grad_ref, keep_ref, mate_ref, send_ref, total_ref):
    grad = halves(grad_ref[...])
    for i in range(4):
        rows = slice(512 * i, 512 * i + 512)
        total_ref[rows] = product(halves(expanded_ref[:, rows]), grad, ((0,), (0,)))
    for i, to_ref in enumerate((keep_ref, mate_ref)):
        for z in range(8):
            j = (place_ref[0] ^ i) * 8 + z
            split_cores(place_ref[1], total_ref, j, 64, to_ref, send_ref, z, (i, z))


def share_parts(yl, c, expanded, grad):
    return pl.pallas_call(
        share_kernel,
        in_specs=[SMEM, VMEM, VMEM],
        out_specs=[VMEM] * 3,
        out_shape=split_shapes(64),
        scratch_shapes=[pltpu.VMEM((2048, 384), f32)],
        compiler_params=pltpu.CompilerParams(vmem_limit_bytes=24 * MIB),
        cost_estimate=pl.CostEstimate(
            flops=6 * 160 * 2048 * 384, bytes_accessed=6 * MIB, transcendentals=0
        ),
    )(jnp.stack([yl, c]).astype(jnp.int32), expanded, grad)


def blocks_kernel(a_ref, b_ref, out_ref):
    a = halves(a_ref[...])
    n, m = a[0].shape[0], out_ref.shape[2]
    for q in range(8):
        b = b_ref[q * m : q * m + m, :]
        if b.dtype == bf16:
            total = sum(
                lax.dot_general(u, b, (((1,), (1,)), ((), ())), preferred_element_type=f32) for u in a
            )
        else:
            total = product(a, halves(b), ((1,), (1,)))
        out_ref[q, :n] = total
        out_ref[q, n:] = with_top(total, PAD)


def blocks_of(a, b):
    n, m = a.shape[0], b.shape[0] // 8
    return pl.pallas_call(
        blocks_kernel,
        in_specs=[VMEM, VMEM],
        out_specs=VMEM,
        out_shape=jax.ShapeDtypeStruct((8, n + PAD, m), f32),
        compiler_params=pltpu.CompilerParams(vmem_limit_bytes=24 * MIB),
        cost_estimate=pl.CostEstimate(
            flops=6 * a.shape[0] * b.size, bytes_accessed=6 * MIB, transcendentals=0
        ),
    )(a, b)


def shards(tokens, cotangent, teacher, expand_model, expand_heads):
    yl, z, c = [lax.axis_index(name) for name in ROW]
    yh, x = [lax.axis_index(name) for name in COL]

    packed = pair_y(pack_teacher_heads(teacher, expand_heads.T), yl)
    tokens_late = after(tokens, packed)
    sent, own = sum_mates(*weight_parts(yl, c, tokens_late, cotangent))
    packed = after(gather_z(packed), sent)
    model_two = after(pair_col(expand_model), sent)

    shapes = [jax.ShapeDtypeStruct((32, 128, 256), bf16), jax.ShapeDtypeStruct((32, 64, 384), f32)]
    teacher_block, heads = weave(packed, c, shapes, put_teacher_heads)
    teacher_block, heads = teacher_block.reshape(4096, 256), heads.reshape(2048, 384)
    model_rows = gather_col(model_two, yh, x)
    expanded_two = pair_col(jnp.dot(model_rows, teacher_block.astype(f32), precision=HIGH))
    expanded = gather_col(expanded_two, yh, x)
    blocks = lax.all_to_all(blocks_z(sent, own), "z", 0, 0, tiled=True)

    student = jnp.dot(expanded, heads, precision=HIGH).astype(bf16)
    student_two = pair_y(student, yl)
    student_own = gather_z(student_two)

    grad = jnp.sum(dec(after(blocks, student_two)), axis=0)
    sent, own = sum_mates(*share_parts(yl, c, expanded, grad))
    side = swap_col(payload(blocks_of(grad, heads)))
    side = jnp.sum(dec(after(side, sent, student_two)), axis=0)
    blocks = payload(blocks_of(side, teacher_block))
    grad_model = jnp.sum(dec(swap_col(blocks)), axis=0)
    shares = parts_z(after(blocks_z(sent, own), blocks), z)
    grad_heads = sum(dec(p) for p in shares).T

    shape = jax.ShapeDtypeStruct((32, 160, 384), bf16)
    student = weave(after(student_own, blocks), c, shape, put_rows, 4).reshape(5120, 384)
    queries = jnp.dot(tokens, student, preferred_element_type=f32)
    return (queries, grad_model, grad_heads)


def solution(mesh):
    mesh = Mesh(mesh.devices.reshape(2, 8, 2, 2, 4), ROW + COL)
    in_specs = (P(ROW, None), P(ROW, COL), P(ROW, COL), P(ROW, COL), P(COL, ROW))
    out_specs = (P(ROW, COL), P(ROW, COL), P(COL, ROW))
    return jax.shard_map(
        shards, mesh=mesh, in_specs=in_specs, out_specs=out_specs, check_vma=False
    )
```
